32 devices in a mesh: ctx: 8 (over z, x), head: 4 (over y, core).
Axes of the slice: x: 2, y: 2, z: 4, core: 2. Of those that a mesh axis runs over, the one named last changes fastest.
Arguments:
- queries: bfloat16 [4096, 4096], P('ctx', 'head'), may hold values from -10 to 10
- cache_keys: bfloat16 [4096, 4096], P('ctx', 'head'), may hold values from -6 to 6
- cache_values: bfloat16 [4096, 4096], P('ctx', 'head'), may hold values from -6 to 6
- new_keys: bfloat16 [4096, 4096], P('ctx', 'head'), may hold values from -6 to 6
- new_values: bfloat16 [4096, 4096], P('ctx', 'head'), may hold values from -6 to 6
- chosen: int32 [64, 4], P('ctx'), may hold values from 0 to 7, all different within a row; in each aligned block of 8 rows (0 to 7, 8 to 15, ...) at most 4 rows name the same one
- out_weight: bfloat16 [4096, 8192], P('head'), may hold values from -1 to 1
Outputs:
- projected: bfloat16 [4096, 8192], P('ctx', 'head')
The draws below stay inside these ranges and needn't reach their ends.
Inputs may be any that keep to these rules, and one draw needn't show every extreme that they name: `chosen`: each row names 4 different cached blocks. Among the 8 query blocks of one tile no cached block is named more than 4 times.
All inputs are finite; a program needn't handle non-finite values.
Results may differ from the reference program's by a relative error of at most 0.0095.
Values may be sent and summed in bfloat16 or wider, within the bound.
A program may use at most 128 MiB of HBM per device.

```python
import math
import jax
import jax.numpy as jnp
import numpy as np
from jax import lax

HEADS = 32
HD = 128
D = 8192
BLK = 512
QG = 64
TOPK = 4
GROUPS_DEV = 8
MOST = 4
CACHED = 4096
NQ = 4096
NGROUPS = 64
N_CTX = 8
N_HEAD = 4


def key_like(key, rows):
    drawn = jnp.clip(jax.random.normal(key, (rows, HEADS * HD), jnp.float32), -6.0, 6.0)
    return drawn.astype(jnp.bfloat16)


def draw_queries(key, part):
    key = jax.random.fold_in(key, 1)
    noise_key = jax.random.fold_in(key, 0)
    drawn = jnp.clip(jax.random.normal(noise_key, (NQ, HEADS * HD), jnp.float32), -6.0, 6.0)
    return drawn.astype(jnp.bfloat16)


def draw_cache_keys(key, part):
    key = jax.random.fold_in(key, 2)
    return key_like(key, CACHED)


def draw_new_keys(key, part):
    key = jax.random.fold_in(key, 3)
    return key_like(key, NQ)


def strengthened(result, own_key, source, target, shards_of, factor):
    owner, partner = [(jnp.arange(result.shape[position]) // (result.shape[position] // shards_of)).reshape([-1 if axis == position else 1 for axis in range(result.ndim)]) for position in (source, target)]
    chosen = jax.random.permutation(own_key, shards_of)[partner]
    strong = (owner == chosen) | (owner == (partner + shards_of // 2) % shards_of)
    return jnp.where(strong, factor * result, result)


def levels(stream_key, dims, cuts, smallest, top_value):
    gain = 1.0
    for axis_at, shards_of in cuts:
        draws = jax.random.uniform(jax.random.fold_in(jax.random.fold_in(stream_key, 6), axis_at), (shards_of,), jnp.float32, smallest / len(cuts), top_value / len(cuts))
        gain = gain * jnp.repeat(jnp.exp(draws), dims[axis_at] // shards_of).reshape((-1,) + (1,) * (len(dims) - 1 - axis_at))
    return gain


def routed_block(rng, own, number, rows, count, top, most, lean):
    order = jax.random.permutation(rng, count)
    crowded, ordinary = load_shares(count, rows * top, most, lean, True), load_shares(count, rows * top, most, lean, False)
    places = jnp.arange(count)

    def named(tallies, rotation):
        used = int((tallies > 0).sum())
        fixed = max(1, used // 4)
        moved = fixed + (places - fixed + rotation * (used - fixed)) % max(1, count - fixed)
        return jnp.zeros((count,), jnp.int32).at[order[jnp.where(places < fixed, places, moved)]].set(jnp.asarray(tallies, jnp.int32))

    tallies = jnp.where(number % 4 == 0, named(crowded, number // 4), named(ordinary, number - number // 4 - 1))
    mixed = jax.random.permutation(jax.random.fold_in(own, 3), count)
    giver, taker = mixed[0:count // 2 * 2:2], mixed[1:count // 2 * 2:2]
    slack = jnp.minimum(tallies[giver] - 1, most - tallies[taker]) // 2
    slack = jnp.where((giver == order[0]) | (taker == order[0]) | (tallies[taker] == 0), 0, jnp.maximum(slack, 0))
    moved = jax.random.randint(jax.random.fold_in(own, 4), (count // 2,), 0, 1 << 20) % (slack + 1)
    tallies = tallies.at[giver].add(-moved).at[taker].add(moved)
    labels = jnp.searchsorted(jnp.cumsum(tallies), jnp.arange(rows * top), side="right").astype(jnp.int32)
    table = labels.reshape(top, rows).T
    table = table[jax.random.permutation(jax.random.fold_in(own, 1), rows)]
    rotation = jax.random.randint(jax.random.fold_in(own, 2), (rows, 1), 0, top)
    return jnp.take_along_axis(table, (jnp.arange(top)[None, :] + rotation) % top, axis=1)


def load_shares(number_of, total, most, skew, full):
    portions = [(1 << 20) // math.isqrt(rank ** skew) + 1 for rank in range(1, number_of + 1)]
    largest = most if full else min(most, max(-(-total // number_of), total * portions[0] // sum(portions)))
    least = 1 if total - largest >= number_of - 1 else 0
    counts, surplus = [largest] + [least] * (number_of - 1), total - largest - least * (number_of - 1)
    while surplus > 0:
        movable = [i for i in range(1, number_of) if counts[i] < largest] or [i for i in range(1, number_of) if counts[i] < most]
        mass, remaining = sum([portions[i] for i in movable]), surplus
        for i in movable:
            addition = min(most - counts[i], max(1, remaining * portions[i] // mass), surplus)
            counts[i] = counts[i] + addition
            surplus = surplus - addition
    return np.array(counts)


def gaussian(rng, dims, scale, most, shards=(), kind=jnp.bfloat16):
    entries = jax.random.normal(rng, dims, jnp.float32) * scale
    if len(shards) > 0:
        entries = levels(rng, dims, shards, -0.22, 0.18) * entries
    return jnp.clip(entries, min=-most, max=most).astype(kind)


def gaussian_with(rng, dims, scale, reach, cuts, heavy, kind=jnp.bfloat16):
    values = scale * jax.random.normal(rng, dims, jnp.float32)
    if cuts:
        values = values * levels(rng, dims, cuts, -0.22, 0.18)
    return jnp.clip(strengthened(values, jax.random.fold_in(rng, 3), *heavy), -reach, reach).astype(kind)


def setup_inputs(seed: int = 0) -> dict:
    splits = jax.random.split(jax.random.key(seed), 8)
    queries = draw_queries(jax.random.fold_in(splits[7], 71), 0)
    cache_keys = draw_cache_keys(jax.random.fold_in(splits[7], 71), 0)
    cache_values = gaussian(splits[2], (CACHED, HEADS * HD), 1.0, 6.0, ((0, 8), (1, 4)))
    new_keys = draw_new_keys(jax.random.fold_in(splits[7], 71), 0)
    new_values = gaussian(splits[4], (NQ, HEADS * HD), 1.0, 6.0, ((0, 8), (1, 4)))
    chosen_keys = jax.random.split(jax.random.fold_in(splits[5], 1), NGROUPS // GROUPS_DEV)
    chosen_turns = jax.random.permutation(jax.random.fold_in(splits[5], 3), NGROUPS // GROUPS_DEV)
    chosen = jax.vmap(lambda own, number: routed_block(jax.random.fold_in(splits[5], 2), own, number, GROUPS_DEV, N_CTX, TOPK, MOST, 2))(chosen_keys, chosen_turns).reshape((NGROUPS, TOPK))
    out_weight = gaussian_with(splits[6], (HEADS * HD, D), 0.2, 1.0, ((0, 4),), (0, 1, 4, 2.0))
    return dict(queries=queries, cache_keys=cache_keys, cache_values=cache_values, new_keys=new_keys, new_values=new_values, chosen=chosen, out_weight=out_weight)


def attend(query_rows, key_rows, value_rows, visible):
    scores = jnp.einsum('rhd,shd->hrs', query_rows.astype(jnp.float32), key_rows.astype(jnp.float32)) / math.sqrt(HD)
    if visible is not None:
        scores = jnp.where(visible[None], scores, jnp.float32(-1e+30))
    row_max = lax.optimization_barrier(jnp.max(scores, axis=-1, keepdims=True))
    weights = jnp.exp(scores - row_max)
    row_total = lax.optimization_barrier(jnp.sum(weights, axis=-1, keepdims=True))
    probs = (weights / row_total).astype(jnp.bfloat16)
    partial_value = jnp.einsum('hrs,shd->rhd', probs.astype(jnp.float32), value_rows.astype(jnp.float32)).astype(jnp.bfloat16)
    log_total = jnp.transpose((row_max + jnp.log(row_total))[..., 0])
    return (partial_value, log_total)

def combine(partials, log_totals):
    top_log = lax.optimization_barrier(jnp.max(log_totals, axis=0, keepdims=True))
    weights = jnp.exp(log_totals - top_log)
    row_total = lax.optimization_barrier(jnp.sum(weights, axis=0))
    merged = lax.optimization_barrier(jnp.sum(weights[..., None] * partials.astype(jnp.float32), axis=0)) / row_total[..., None]
    return merged.astype(jnp.bfloat16)

def reference(queries, cache_keys, cache_values, new_keys, new_values, chosen, out_weight):
    heads = queries.shape[1] // HD
    groups = BLK // QG
    query_tiles = queries.reshape(N_CTX, BLK, heads, HD)
    new_key_tiles = new_keys.reshape(N_CTX, BLK, heads, HD)
    new_value_tiles = new_values.reshape(N_CTX, BLK, heads, HD)
    cache_key_blocks = cache_keys.reshape(N_CTX, BLK, heads, HD)
    cache_value_blocks = cache_values.reshape(N_CTX, BLK, heads, HD)
    chosen_tiles = chosen.reshape(N_CTX, groups, TOPK)
    positions = jnp.arange(BLK, dtype=jnp.int32)
    visible = positions[:, None] >= positions[None, :]

    def one_block(inputs):
        group_query, block_index = inputs
        key_block = lax.dynamic_index_in_dim(cache_key_blocks, block_index.astype(jnp.int32), 0, keepdims=False)
        value_block = lax.dynamic_index_in_dim(cache_value_blocks, block_index.astype(jnp.int32), 0, keepdims=False)
        return attend(group_query, key_block, value_block, None)

    def one_group(inputs):
        group_query, group_picks, group_own, group_log = inputs
        remote, remote_log = lax.map(one_block, (jnp.broadcast_to(group_query, (TOPK,) + group_query.shape), group_picks))
        partials = jnp.concatenate([group_own[None], remote], axis=0)
        log_totals = jnp.concatenate([group_log[None], remote_log], axis=0)
        return combine(partials, log_totals)

    def one_tile(inputs):
        query_tile, key_tile, value_tile, picks = inputs
        own_part, own_log = attend(query_tile, key_tile, value_tile, visible)
        merged = lax.map(one_group, (query_tile.reshape(groups, QG, heads, HD), picks, own_part.reshape(groups, QG, heads, HD), own_log.reshape(groups, QG, heads)))
        return merged.reshape(BLK, heads * HD)
    attention = lax.map(one_tile, (query_tiles, new_key_tiles, new_value_tiles, chosen_tiles)).reshape(N_CTX * BLK, heads * HD)
    width = heads * HD // N_HEAD

    def add_group(carry, group_index):
        start = (group_index * width).astype(jnp.int32)
        columns = lax.dynamic_slice_in_dim(attention, start, width, 1)
        weight_rows = lax.dynamic_slice_in_dim(out_weight, start, width, 0)
        term = jnp.dot(columns, weight_rows, preferred_element_type=jnp.float32).astype(jnp.bfloat16)
        term = lax.optimization_barrier(term)
        return (carry + term.astype(jnp.float32), None)
    start_sum = jnp.zeros((attention.shape[0], out_weight.shape[1]), jnp.float32)
    summed, unused = lax.scan(add_group, start_sum, jnp.arange(N_HEAD, dtype=jnp.int32))
    return summed.astype(jnp.bfloat16)
```

```python
import functools
import math

import jax
import jax.numpy as jnp
from jax import lax
from jax.experimental import pallas as pl
from jax.experimental.pallas import tpu as pltpu
from jax.sharding import PartitionSpec as P

HD = 128
QG = 64
TOPK = 4
MESH = pl.DeviceIdType.MESH


def project_kernel(
    n_y, a_ref, w_ref, out_ref, w_buf, pair_out, pair_in, held, far_out, far_in,
    w_sem, pair_send, pair_recv, far_send, far_recv,
):
    head = lax.axis_index("head")
    core = lax.rem(head, 2)
    row = head // 2
    partner = head + 1 - 2 * core
    steps, _, tile = held.shape
    tiles = steps // n_y
    far = (n_y - 1) * tiles
    share = tiles * tile

    def w_copy(step, which):
        to_row = lax.rem(row + 1 + step // tiles, n_y)
        to_core = core if which else 1 - core
        start = (to_row * 2 + to_core) * share + lax.rem(step, tiles) * tile
        return pltpu.make_async_copy(
            w_ref.at[:, pl.ds(pl.multiple_of(start, tile), tile)],
            w_buf.at[which, step],
            w_sem.at[which, step],
        )

    def pair_copy(step):
        return pltpu.make_async_remote_copy(
            src_ref=pair_out.at[step], dst_ref=pair_in.at[step],
            send_sem=pair_send.at[step], recv_sem=pair_recv.at[step],
            device_id={"head": partner}, device_id_type=MESH,
        )

    def far_copy(step):
        to_row = lax.rem(row + 1 + step // tiles, n_y)
        return pltpu.make_async_remote_copy(
            src_ref=far_out.at[step], dst_ref=far_in.at[step],
            send_sem=far_send.at[step], recv_sem=far_recv.at[step],
            device_id={"head": to_row * 2 + core}, device_id_type=MESH,
        )

    @pl.loop(0, steps)
    def _(step):
        w_copy(step, 0).start()
        w_copy(step, 1).start()

    barrier = pltpu.get_barrier_semaphore()
    pl.semaphore_signal(barrier, inc=1, device_id={"head": partner}, device_id_type=MESH)
    for k in range(1, n_y):
        pl.semaphore_signal(
            barrier, inc=1, device_id={"head": lax.rem(row + k, n_y) * 2 + core},
            device_id_type=MESH,
        )
    pl.semaphore_wait(barrier, n_y)

    def finish(step):
        pair_copy(step).wait_recv()
        far_out[step] = (held[step] + pair_in[step].astype(jnp.float32)).astype(far_out.dtype)
        far_copy(step).start()

    @pl.loop(0, steps)
    def _(step):
        w_copy(step, 0).wait()
        pair_out[step] = jnp.dot(
            a_ref[...], w_buf[0, step], preferred_element_type=jnp.float32
        ).astype(pair_out.dtype)
        pair_copy(step).start()
        w_copy(step, 1).wait()
        held[step] = jnp.dot(a_ref[...], w_buf[1, step], preferred_element_type=jnp.float32)

        @pl.when((step >= 1) & (step <= far))
        def _():
            finish(step - 1)

    for j in range(tiles):
        pair_copy(far + j).wait_recv()
        total = held[far + j] + pair_in[far + j].astype(jnp.float32)
        for k in range(n_y - 1):
            far_copy(k * tiles + j).wait_recv()
            total = total + far_in[k * tiles + j].astype(jnp.float32)
        out_ref[:, j * tile : (j + 1) * tile] = total.astype(out_ref.dtype)

    @pl.loop(0, steps)
    def _(step):
        pair_copy(step).wait_send()

    @pl.loop(0, far)
    def _(step):
        far_copy(step).wait_send()


def project(merged, out_weight):
    rows, depth = merged.shape
    width = out_weight.shape[1]
    n_head = lax.axis_size("head")
    n_y = n_head // 2
    share = width // n_head
    tile = min(512, share)
    tiles = share // tile
    steps = n_y * tiles
    far = (n_y - 1) * tiles
    bf16 = jnp.bfloat16
    dma = pltpu.SemaphoreType.DMA
    return pl.pallas_call(
        functools.partial(project_kernel, n_y),
        out_shape=jax.ShapeDtypeStruct((rows, share), bf16),
        in_specs=[
            pl.BlockSpec(memory_space=pltpu.VMEM),
            pl.BlockSpec(memory_space=pl.ANY),
        ],
        out_specs=pl.BlockSpec(memory_space=pltpu.VMEM),
        scratch_shapes=[
            pltpu.VMEM((2, steps, depth, tile), bf16),
            pltpu.VMEM((steps, rows, tile), bf16),
            pltpu.VMEM((steps, rows, tile), bf16),
            pltpu.VMEM((steps, rows, tile), jnp.float32),
            pltpu.VMEM((far, rows, tile), bf16),
            pltpu.VMEM((far, rows, tile), bf16),
            dma((2, steps)), dma((steps,)), dma((steps,)), dma((far,)), dma((far,)),
        ],
        compiler_params=pltpu.CompilerParams(
            collective_id=1, has_side_effects=True, vmem_limit_bytes=56 * 1024 * 1024
        ),
        cost_estimate=pl.CostEstimate(
            flops=2 * rows * depth * width, bytes_accessed=2 * depth * width, transcendentals=0
        ),
    )(merged, out_weight)


def attend(query_rows, key_rows, value_rows, visible):
    partials = []
    log_totals = []
    for head_number in range(query_rows.shape[1]):
        scores = lax.dot_general(
            query_rows[:, head_number],
            key_rows[:, head_number],
            (((1,), (1,)), ((), ())),
            preferred_element_type=jnp.float32,
        ) / math.sqrt(HD)
        if visible is not None:
            scores = jnp.where(visible, scores, jnp.float32(-1e30))
        row_max = jnp.max(scores, axis=-1, keepdims=True)
        weights = jnp.exp(scores - row_max)
        row_total = jnp.sum(weights, axis=-1, keepdims=True)
        probs = (weights / row_total).astype(jnp.bfloat16)
        partial_value = jnp.dot(
            probs, value_rows[:, head_number], preferred_element_type=jnp.float32
        )
        partials.append(partial_value.astype(jnp.bfloat16))
        log_totals.append((row_max + jnp.log(row_total))[:, 0])
    return (jnp.stack(partials, axis=1), jnp.stack(log_totals, axis=1))


def pack_slots(queries, slot_index, live, slot_total, groups, ctx_size, capacity, head_count):
    pair_total = slot_index.shape[0]
    slot_pick = (
        (jnp.arange(slot_total, dtype=jnp.int32)[:, None] == slot_index[None, :]) & live[None, :]
    ).astype(jnp.bfloat16)
    pair_group = jnp.arange(pair_total, dtype=jnp.int32) // TOPK
    group_pick = (pair_group[:, None] == jnp.arange(groups, dtype=jnp.int32)[None, :]).astype(
        jnp.bfloat16
    )
    slot_group = jnp.dot(slot_pick, group_pick, preferred_element_type=jnp.float32).astype(
        jnp.bfloat16
    )
    outgoing = jnp.dot(slot_group, queries.reshape(groups, -1), preferred_element_type=jnp.float32)
    return outgoing.astype(jnp.bfloat16).reshape(ctx_size, capacity, QG, head_count, HD)


def on_device(queries, cache_keys, cache_values, new_keys, new_values, chosen, out_weight):
    block_len = queries.shape[0]
    head_count = queries.shape[1] // HD
    groups = block_len // QG
    ctx_size = lax.axis_size("ctx")
    capacity = max(2, (groups * TOPK + ctx_size - 1) // ctx_size)
    query_rows = queries.reshape(block_len, head_count, HD)
    key_rows = cache_keys.reshape(block_len, head_count, HD)
    value_rows = cache_values.reshape(block_len, head_count, HD)
    target = chosen.reshape(-1)
    pair_total = target.shape[0]
    target_hit = (target[:, None] == jnp.arange(ctx_size, dtype=jnp.int32)[None, :]).astype(
        jnp.int32
    )
    before = jnp.sum((jnp.cumsum(target_hit, axis=0) - target_hit) * target_hit, axis=1)
    every_pair = jnp.ones((pair_total,), bool)
    slot_total = ctx_size * capacity
    slot_of = target * capacity + before
    outgoing = pack_slots(
        queries, slot_of, every_pair, slot_total, groups, ctx_size, capacity, head_count
    )
    incoming = lax.all_to_all(outgoing, "ctx", split_axis=0, concat_axis=0, tiled=True)
    item_count = incoming.shape[1]
    flat_rows = incoming.reshape(-1, head_count, HD)
    partial_value, log_total = attend(flat_rows, key_rows, value_rows, None)
    partial_value = partial_value.reshape(ctx_size, item_count, QG, head_count, HD)
    log_total = log_total.reshape(ctx_size, item_count, QG, head_count)
    partial_value, log_total = (partial_value, log_total)
    arrived = lax.all_to_all(
        partial_value.astype(jnp.float32), "ctx", split_axis=0, concat_axis=0, tiled=True
    ).astype(partial_value.dtype)
    arrived_log = lax.all_to_all(log_total, "ctx", split_axis=0, concat_axis=0, tiled=True)
    remote = jnp.take(arrived.reshape(slot_total, -1), slot_of, axis=0)
    remote_log = jnp.take(arrived_log.reshape(slot_total, -1), slot_of, axis=0)
    positions = jnp.arange(block_len, dtype=jnp.int32)
    visible = positions[:, None] >= positions[None, :]
    own_part, own_log = attend(
        query_rows,
        new_keys.reshape(block_len, head_count, HD),
        new_values.reshape(block_len, head_count, HD),
        visible,
    )
    remote = remote.reshape(groups, TOPK, QG, head_count, HD)
    remote_log = remote_log.reshape(groups, TOPK, QG, head_count)
    partials = jnp.concatenate([own_part.reshape(groups, 1, QG, head_count, HD), remote], axis=1)
    log_totals = jnp.concatenate([own_log.reshape(groups, 1, QG, head_count), remote_log], axis=1)
    top_log = jnp.max(log_totals, axis=1, keepdims=True)
    weights = jnp.exp(log_totals - top_log)
    row_total = jnp.sum(weights, axis=1)
    merged = (
        jnp.sum(weights[..., None] * partials.astype(jnp.float32), axis=1) / row_total[..., None]
    )
    merged = merged.astype(jnp.bfloat16).reshape(block_len, head_count * HD)
    return project(merged, out_weight)


def solution(mesh):
    placed = (
        P("ctx", "head"),
        P("ctx", "head"),
        P("ctx", "head"),
        P("ctx", "head"),
        P("ctx", "head"),
        P("ctx", None),
        P("head", None),
    )
    return jax.shard_map(
        on_device, mesh=mesh, in_specs=placed, out_specs=P("ctx", "head"), check_vma=False
    )
```

```python
import functools
import math

import jax
import jax.numpy as jnp
from jax import lax
from jax.experimental import pallas as pl
from jax.experimental.pallas import tpu as pltpu
from jax.sharding import PartitionSpec as P

HD = 128
QG = 64
TOPK = 4
MESH = pl.DeviceIdType.MESH


def project_kernel(
    n_y, a_ref, w_ref, out_ref, w_buf, pair_out, pair_in, held, far_out, far_in,
    w_sem, pair_send, pair_recv, far_send, far_recv,
):
    head = lax.axis_index("head")
    core = lax.rem(head, 2)
    row = head // 2
    partner = head + 1 - 2 * core
    steps, _, tile = held.shape
    tiles = steps // n_y
    far = (n_y - 1) * tiles
    share = tiles * tile

    def w_copy(step, which):
        to_row = lax.rem(row + 1 + step // tiles, n_y)
        to_core = core if which else 1 - core
        start = (to_row * 2 + to_core) * share + lax.rem(step, tiles) * tile
        return pltpu.make_async_copy(
            w_ref.at[:, pl.ds(pl.multiple_of(start, tile), tile)],
            w_buf.at[which, step],
            w_sem.at[which, step],
        )

    def pair_copy(step):
        return pltpu.make_async_remote_copy(
            src_ref=pair_out.at[step], dst_ref=pair_in.at[step],
            send_sem=pair_send.at[step], recv_sem=pair_recv.at[step],
            device_id={"head": partner}, device_id_type=MESH,
        )

    def far_copy(step):
        to_row = lax.rem(row + 1 + step // tiles, n_y)
        return pltpu.make_async_remote_copy(
            src_ref=far_out.at[step], dst_ref=far_in.at[step],
            send_sem=far_send.at[step], recv_sem=far_recv.at[step],
            device_id={"head": to_row * 2 + core}, device_id_type=MESH,
        )

    @pl.loop(0, steps)
    def _(step):
        w_copy(step, 0).start()
        w_copy(step, 1).start()

    barrier = pltpu.get_barrier_semaphore()
    pl.semaphore_signal(barrier, inc=1, device_id={"head": partner}, device_id_type=MESH)
    for k in range(1, n_y):
        pl.semaphore_signal(
            barrier, inc=1, device_id={"head": lax.rem(row + k, n_y) * 2 + core},
            device_id_type=MESH,
        )
    pl.semaphore_wait(barrier, n_y)

    def finish(step):
        pair_copy(step).wait_recv()
        far_out[step] = (held[step] + pair_in[step].astype(jnp.float32)).astype(far_out.dtype)
        far_copy(step).start()

    @pl.loop(0, steps)
    def _(step):
        w_copy(step, 0).wait()
        pair_out[step] = jnp.dot(
            a_ref[...], w_buf[0, step], preferred_element_type=jnp.float32
        ).astype(pair_out.dtype)
        pair_copy(step).start()
        w_copy(step, 1).wait()
        held[step] = jnp.dot(a_ref[...], w_buf[1, step], preferred_element_type=jnp.float32)

        @pl.when((step >= 1) & (step <= far))
        def _():
            finish(step - 1)

    for j in range(tiles):
        pair_copy(far + j).wait_recv()
        total = held[far + j] + pair_in[far + j].astype(jnp.float32)
        for k in range(n_y - 1):
            far_copy(k * tiles + j).wait_recv()
            total = total + far_in[k * tiles + j].astype(jnp.float32)
        out_ref[:, j * tile : (j + 1) * tile] = total.astype(out_ref.dtype)

    @pl.loop(0, steps)
    def _(step):
        pair_copy(step).wait_send()

    @pl.loop(0, far)
    def _(step):
        far_copy(step).wait_send()


def project(merged, out_weight):
    rows, depth = merged.shape
    width = out_weight.shape[1]
    n_head = lax.axis_size("head")
    n_y = n_head // 2
    share = width // n_head
    tile = min(512, share)
    tiles = share // tile
    steps = n_y * tiles
    far = (n_y - 1) * tiles
    bf16 = jnp.bfloat16
    dma = pltpu.SemaphoreType.DMA
    return pl.pallas_call(
        functools.partial(project_kernel, n_y),
        out_shape=jax.ShapeDtypeStruct((rows, share), bf16),
        in_specs=[
            pl.BlockSpec(memory_space=pltpu.VMEM),
            pl.BlockSpec(memory_space=pl.ANY),
        ],
        out_specs=pl.BlockSpec(memory_space=pltpu.VMEM),
        scratch_shapes=[
            pltpu.VMEM((2, steps, depth, tile), bf16),
            pltpu.VMEM((steps, rows, tile), bf16),
            pltpu.VMEM((steps, rows, tile), bf16),
            pltpu.VMEM((steps, rows, tile), jnp.float32),
            pltpu.VMEM((far, rows, tile), bf16),
            pltpu.VMEM((far, rows, tile), bf16),
            dma((2, steps)), dma((steps,)), dma((steps,)), dma((far,)), dma((far,)),
        ],
        compiler_params=pltpu.CompilerParams(
            collective_id=1, has_side_effects=True, vmem_limit_bytes=56 * 1024 * 1024
        ),
        cost_estimate=pl.CostEstimate(
            flops=2 * rows * depth * width, bytes_accessed=2 * depth * width, transcendentals=0
        ),
    )(merged, out_weight)


def pack_kernel(q_ref, chosen_ref, pack_ref, spread_ref):
    groups = chosen_ref.shape[0]
    chunks, slot_rows, width = pack_ref.shape[2:]
    rows = q_ref.shape[0]
    slots = slot_rows // QG
    me = lax.axis_index("ctx")
    z, x = me // 2, lax.rem(me, 2)
    half = z // 2
    z_of = (1 + half, 3 * half, 2 - half, 3 - 3 * half)
    row_at = lax.broadcasted_iota(jnp.int32, (QG, rows), 0)
    col_at = lax.broadcasted_iota(jnp.int32, (QG, rows), 1)
    for col in range(2):
        for r in range(4):
            block = z_of[r] * 2 + (x if col == 0 else 1 - x)
            found = [jnp.int32(-1)] * slots
            count = jnp.int32(0)
            for g in range(groups):
                hit = jnp.int32(0)
                for k in range(TOPK):
                    hit = hit + (chosen_ref[g, k] == block).astype(jnp.int32)
                for s in range(slots):
                    found[s] = jnp.where((hit > 0) & (count == s), g, found[s])
                count = count + hit
            for s in range(slots):
                at = slice(s * QG, (s + 1) * QG)
                start = pl.multiple_of(jnp.maximum(found[s], 0) * QG, QG)
                for c in range(chunks):
                    pack_ref[col, r, c, at, :] = q_ref[
                        pl.ds(start, QG), c * width : (c + 1) * width
                    ]
                spread_ref[col, r, at, :] = jnp.where(
                    (col_at == row_at + start) & (found[s] >= 0), 1.0, 0.0
                ).astype(jnp.bfloat16)


def attention_kernel(
    q_ref, key_ref, value_ref, new_key_ref, new_value_ref, q_pack, spreads, merged_ref,
    keys, values, q_side, q_end, o_side, o_end, o_home, l_side, l_end, l_home,
    own_o, own_l, shares,
    load_sem, kv_send, kv_recv, q_send, side_q_recv, end_q_recv,
    side_o_send, end_o_send, o_recv, side_l_send, end_l_send, l_recv,
):
    chunks, _, width = keys.shape[1:]
    slot_rows = q_pack.shape[3]
    rows = q_ref.shape[0]
    per_chunk = width // HD
    scale = 1.0 / math.sqrt(HD)

    me = lax.axis_index("ctx")
    z, x = me // 2, lax.rem(me, 2)
    half = z // 2
    z_of = (1 + half, 3 * half, 2 - half, 3 - 3 * half)
    is_mid = (z == 1) | (z == 2)
    is_end = (z == 0) | (z == 3)
    own = jnp.where(is_mid, 0, 1)
    side = z * 2 + 1 - x
    pair_z = z_of[0] + z_of[1] - z
    pair, pair_across = pair_z * 2 + x, pair_z * 2 + 1 - x
    beyond = z_of[2] * 2 + x

    def remote(src, dst, send_sem, recv_sem, to):
        return pltpu.make_async_remote_copy(
            src_ref=src, dst_ref=dst, send_sem=send_sem, recv_sem=recv_sem,
            device_id={"ctx": to}, device_id_type=MESH,
        )

    def load(c, which):
        ref, held = ((key_ref, keys), (value_ref, values))[which]
        return pltpu.make_async_copy(
            ref.at[:, pl.ds(pl.multiple_of(c * width, width), width)],
            held.at[own, c], load_sem.at[c, which],
        )

    def kv_copy(kind, c, which):
        held = (keys, values)[which]
        src = 1 if kind == 2 else own
        dst = (own, 2, 3)[kind]
        return remote(
            held.at[src, c], held.at[dst, c], kv_send.at[kind, c, which],
            kv_recv.at[dst, c, which], pair if kind == 0 else beyond,
        )

    def side_q(r, c):
        return remote(
            q_pack.at[1, r, c], q_side.at[r, c], q_send.at[1, r, c], side_q_recv.at[r, c], side
        )

    def end_q(col, r, c):
        return remote(
            q_pack.at[col, r, c], q_end.at[col, r - 2, c], q_send.at[col, r, c],
            end_q_recv.at[col, r - 2, c], (pair, pair_across)[col],
        )

    def side_o(r, c):
        return remote(
            o_side.at[r, c], o_home.at[1, r, c], side_o_send.at[r, c], o_recv.at[1, r, c], side
        )

    def side_l(r):
        return remote(l_side.at[r], l_home.at[1, r], side_l_send.at[r], l_recv.at[1, r], side)

    def end_o(col, r, c):
        return remote(
            o_end.at[col, r - 2, c], o_home.at[col, r, c], end_o_send.at[col, r - 2, c],
            o_recv.at[col, r, c], (pair, pair_across)[col],
        )

    def end_l(col, r):
        return remote(
            l_end.at[col, r - 2], l_home.at[col, r], end_l_send.at[col, r - 2],
            l_recv.at[col, r], (pair, pair_across)[col],
        )

    for c in range(chunks):
        load(c, 0).start()
        load(c, 1).start()

    barrier = pltpu.get_barrier_semaphore()
    for to in (side, pair, pair_across):
        pl.semaphore_signal(barrier, inc=1, device_id={"ctx": to}, device_id_type=MESH)

    @pl.when(is_mid)
    def _():
        pl.semaphore_signal(barrier, inc=1, device_id={"ctx": beyond}, device_id_type=MESH)

    @pl.when(is_mid)
    def _():
        pl.semaphore_wait(barrier, 4)

    @pl.when(is_end)
    def _():
        pl.semaphore_wait(barrier, 3)

    @pl.when(is_end)
    def _():
        for c in range(chunks):
            end_q(0, 2, c).start()
            end_q(1, 2, c).start()

    @pl.loop(0, 2)
    def _(r):
        @pl.loop(0, chunks)
        def _(c):
            side_q(r, c).start()

    @pl.loop(0, chunks)
    def _(c):
        for which in range(2):
            load(c, which).wait()
            kv_copy(0, c, which).start()

        @pl.when(is_mid)
        def _():
            for which in range(2):
                kv_copy(1, c, which).start()

        @pl.when(is_end)
        def _():
            end_q(0, 3, c).start()
            end_q(1, 3, c).start()

    @pl.when(is_mid)
    def _():
        @pl.loop(2, 4)
        def _(r):
            @pl.loop(0, chunks)
            def _(c):
                side_q(r, c).start()

    def attend_one(q, k, v, first):
        scores = lax.dot_general(
            k, q, (((1,), (1,)), ((), ())), preferred_element_type=jnp.float32
        )
        if first is not None:
            key_at = lax.broadcasted_iota(jnp.int32, scores.shape, 0)
            query_at = lax.broadcasted_iota(jnp.int32, scores.shape, 1) + first
            scores = jnp.where(key_at <= query_at, scores, jnp.float32(-1e30))
        top = jnp.max(scores, axis=0, keepdims=True)
        weights = jnp.exp((scores - top) * scale)
        total = jnp.sum(weights, axis=0, keepdims=True)
        out = lax.dot_general(
            v, weights.astype(jnp.bfloat16), (((0,), (0,)), ((), ())),
            preferred_element_type=jnp.float32,
        )
        return (out * (1.0 / total)).astype(jnp.bfloat16), top * scale + jnp.log(total)

    def unit(q, r, c, o_dst, l_dst):
        for i in range(per_chunk):
            at = slice(i * HD, (i + 1) * HD)
            out, log = attend_one(q[:, at], keys[r, c, :, at], values[r, c, :, at], None)
            o_dst[at, :] = out
            l_dst[pl.ds(c * per_chunk + i, 1), :] = log

    @pl.loop(0, chunks * per_chunk)
    def _(h):
        cols = pl.ds(pl.multiple_of(h * HD, HD), HD)
        for first in range(0, rows, slot_rows):
            seen = first + slot_rows
            out, log = attend_one(
                q_ref[first:seen, cols], new_key_ref[:seen, cols], new_value_ref[:seen, cols], first
            )
            own_o[h, :, first:seen] = out
            own_l[pl.ds(h, 1), first:seen] = log

    @pl.loop(0, jnp.where(is_mid, 4, 2) * chunks)
    def _(step):
        turn, c = step // chunks, lax.rem(step, chunks)
        r = jnp.where(turn == 0, own, jnp.where(turn == 1, 1 - own, turn))

        @pl.when(turn > 0)
        def _():
            for which in range(2):
                held = (keys, values)[which].at[r, c]
                remote(held, held, kv_send.at[0, c, which], kv_recv.at[r, c, which], pair).wait_recv()

        @pl.when(is_mid & (turn == 1))
        def _():
            for which in range(2):
                kv_copy(2, c, which).start()

        unit(q_pack.at[0, r, c], r, c, o_home.at[0, r, c], l_home.at[0, r])
        side_q(r, c).wait_recv()
        unit(q_side.at[r, c], r, c, o_side.at[r, c], l_side.at[r])
        side_o(r, c).start()

        @pl.when(c == chunks - 1)
        def _():
            side_l(r).start()

        @pl.when(turn >= 2)
        def _():
            for col in range(2):
                end_q(col, r, c).wait_recv()
                unit(q_end.at[col, r - 2, c], r, c, o_end.at[col, r - 2, c], l_end.at[col, r - 2])
                end_o(col, r, c).start()

                @pl.when(c == chunks - 1)
                def _():
                    end_l(col, r).start()

    @pl.loop(0, 4)
    def _(r):
        side_l(r).wait_recv()

        @pl.loop(0, chunks)
        def _(c):
            side_o(r, c).wait_recv()

    @pl.when(is_end)
    def _():
        @pl.loop(2, 4)
        def _(r):
            end_l(0, r).wait_recv()

            @pl.loop(0, chunks)
            def _(c):
                end_o(0, r, c).wait_recv()

    logs = []
    for n in range(8):
        placed = spreads[n // 4, n % 4]
        rest = l_home[n // 4, n % 4]
        log = jnp.zeros((rest.shape[0], rows), jnp.float32)
        for _ in range(3):
            piece = rest.astype(jnp.bfloat16)
            rest = rest - piece.astype(jnp.float32)
            log = log + jnp.dot(piece, placed, preferred_element_type=jnp.float32)
        hit = jnp.sum(placed.astype(jnp.float32), axis=0, keepdims=True)
        logs.append(jnp.where(hit > 0, log, jnp.float32(-1e30)))
    logs.append(own_l[...])
    top = functools.reduce(jnp.maximum, logs)
    weights = [jnp.exp(log - top) for log in logs]
    inverse = 1.0 / functools.reduce(jnp.add, weights)
    for n, weight in enumerate(weights):
        shares[n] = weight * inverse

    for c in range(chunks):
        heads = range(c * per_chunk, (c + 1) * per_chunk)
        total = [own_o[h].astype(jnp.float32) * shares[8, h : h + 1, :] for h in heads]
        for n in range(8):
            part = jnp.dot(
                o_home[n // 4, n % 4, c], spreads[n // 4, n % 4],
                preferred_element_type=jnp.float32,
            )
            for i, h in enumerate(heads):
                total[i] = total[i] + part[i * HD : (i + 1) * HD] * shares[n, h : h + 1, :]
        for i, h in enumerate(heads):
            merged_ref[:, h * HD : (h + 1) * HD] = total[i].T.astype(merged_ref.dtype)

    @pl.loop(0, chunks)
    def _(c):
        for which in range(2):
            kv_copy(0, c, which).wait_send()

        @pl.loop(0, 2)
        def _(r):
            side_q(r, c).wait_send()
            side_o(r, c).wait_send()

        @pl.when(is_mid)
        def _():
            for which in range(2):
                kv_copy(1, c, which).wait_send()
                kv_copy(2, c, which).wait_send()

            @pl.loop(2, 4)
            def _(r):
                side_q(r, c).wait_send()
                side_o(r, c).wait_send()
                for col in range(2):
                    end_o(col, r, c).wait_send()

        @pl.when(is_end)
        def _():
            @pl.loop(2, 4)
            def _(r):
                for col in range(2):
                    end_q(col, r, c).wait_send()

    @pl.loop(0, 2)
    def _(r):
        side_l(r).wait_send()

    @pl.when(is_mid)
    def _():
        @pl.loop(2, 4)
        def _(r):
            side_l(r).wait_send()
            for col in range(2):
                end_l(col, r).wait_send()


def attention(queries, cache_keys, cache_values, new_keys, new_values, chosen):
    rows, columns = queries.shape
    heads = columns // HD
    width = min(2 * HD, columns)
    chunks = columns // width
    slot_rows = chosen.size // lax.axis_size("ctx") * QG
    bf16, f32 = jnp.bfloat16, jnp.float32
    dma = pltpu.SemaphoreType.DMA
    in_vmem = pl.BlockSpec(memory_space=pltpu.VMEM)
    in_hbm = pl.BlockSpec(memory_space=pl.ANY)
    work = (slot_rows * 8 + rows) * rows * columns
    packed, spreads = pl.pallas_call(
        pack_kernel,
        out_shape=(
            jax.ShapeDtypeStruct((2, 4, chunks, slot_rows, width), bf16),
            jax.ShapeDtypeStruct((2, 4, slot_rows, rows), bf16),
        ),
        in_specs=[in_vmem, pl.BlockSpec(memory_space=pltpu.SMEM)],
        out_specs=(in_vmem, in_vmem),
        compiler_params=pltpu.CompilerParams(vmem_limit_bytes=24 * 1024 * 1024),
    )(queries, chosen)
    return pl.pallas_call(
        attention_kernel,
        out_shape=jax.ShapeDtypeStruct((rows, columns), bf16),
        in_specs=[
            in_vmem, in_hbm, in_hbm, in_vmem, in_vmem, in_vmem, in_vmem
        ],
        out_specs=in_vmem,
        scratch_shapes=[
            pltpu.VMEM((4, chunks, rows, width), bf16),
            pltpu.VMEM((4, chunks, rows, width), bf16),
            pltpu.VMEM((4, chunks, slot_rows, width), bf16),
            pltpu.VMEM((2, 2, chunks, slot_rows, width), bf16),
            pltpu.VMEM((4, chunks, width, slot_rows), bf16),
            pltpu.VMEM((2, 2, chunks, width, slot_rows), bf16),
            pltpu.VMEM((2, 4, chunks, width, slot_rows), bf16),
            pltpu.VMEM((4, heads, slot_rows), f32),
            pltpu.VMEM((2, 2, heads, slot_rows), f32),
            pltpu.VMEM((2, 4, heads, slot_rows), f32),
            pltpu.VMEM((heads, HD, rows), bf16),
            pltpu.VMEM((heads, rows), f32),
            pltpu.VMEM((9, heads, rows), f32),
            dma((chunks, 2)), dma((3, chunks, 2)), dma((4, chunks, 2)), dma((2, 4, chunks)),
            dma((4, chunks)), dma((2, 2, chunks)),
            dma((4, chunks)), dma((2, 2, chunks)), dma((2, 4, chunks)),
            dma((4,)), dma((2, 2)), dma((2, 4)),
        ],
        compiler_params=pltpu.CompilerParams(
            collective_id=0, has_side_effects=True, vmem_limit_bytes=56 * 1024 * 1024
        ),
        cost_estimate=pl.CostEstimate(
            flops=4 * work, bytes_accessed=12 * rows * columns, transcendentals=work // HD
        ),
    )(queries, cache_keys, cache_values, new_keys, new_values, packed, spreads)


def attend(query_rows, key_rows, value_rows, visible):
    partials = []
    log_totals = []
    for head_number in range(query_rows.shape[1]):
        scores = lax.dot_general(
            query_rows[:, head_number],
            key_rows[:, head_number],
            (((1,), (1,)), ((), ())),
            preferred_element_type=jnp.float32,
        ) / math.sqrt(HD)
        if visible is not None:
            scores = jnp.where(visible, scores, jnp.float32(-1e30))
        row_max = jnp.max(scores, axis=-1, keepdims=True)
        weights = jnp.exp(scores - row_max)
        row_total = jnp.sum(weights, axis=-1, keepdims=True)
        probs = (weights / row_total).astype(jnp.bfloat16)
        partial_value = jnp.dot(
            probs, value_rows[:, head_number], preferred_element_type=jnp.float32
        )
        partials.append(partial_value.astype(jnp.bfloat16))
        log_totals.append((row_max + jnp.log(row_total))[:, 0])
    return (jnp.stack(partials, axis=1), jnp.stack(log_totals, axis=1))


def pack_slots(queries, slot_index, live, slot_total, groups, ctx_size, capacity, head_count):
    pair_total = slot_index.shape[0]
    slot_pick = (
        (jnp.arange(slot_total, dtype=jnp.int32)[:, None] == slot_index[None, :]) & live[None, :]
    ).astype(jnp.bfloat16)
    pair_group = jnp.arange(pair_total, dtype=jnp.int32) // TOPK
    group_pick = (pair_group[:, None] == jnp.arange(groups, dtype=jnp.int32)[None, :]).astype(
        jnp.bfloat16
    )
    slot_group = jnp.dot(slot_pick, group_pick, preferred_element_type=jnp.float32).astype(
        jnp.bfloat16
    )
    outgoing = jnp.dot(slot_group, queries.reshape(groups, -1), preferred_element_type=jnp.float32)
    return outgoing.astype(jnp.bfloat16).reshape(ctx_size, capacity, QG, head_count, HD)


def exchanged_attention(queries, cache_keys, cache_values, new_keys, new_values, chosen):
    block_len = queries.shape[0]
    head_count = queries.shape[1] // HD
    groups = block_len // QG
    ctx_size = lax.axis_size("ctx")
    capacity = max(2, (groups * TOPK + ctx_size - 1) // ctx_size)
    query_rows = queries.reshape(block_len, head_count, HD)
    key_rows = cache_keys.reshape(block_len, head_count, HD)
    value_rows = cache_values.reshape(block_len, head_count, HD)
    target = chosen.reshape(-1)
    pair_total = target.shape[0]
    target_hit = (target[:, None] == jnp.arange(ctx_size, dtype=jnp.int32)[None, :]).astype(
        jnp.int32
    )
    before = jnp.sum((jnp.cumsum(target_hit, axis=0) - target_hit) * target_hit, axis=1)
    every_pair = jnp.ones((pair_total,), bool)
    slot_total = ctx_size * capacity
    slot_of = target * capacity + before
    outgoing = pack_slots(
        queries, slot_of, every_pair, slot_total, groups, ctx_size, capacity, head_count
    )
    incoming = lax.all_to_all(outgoing, "ctx", split_axis=0, concat_axis=0, tiled=True)
    item_count = incoming.shape[1]
    flat_rows = incoming.reshape(-1, head_count, HD)
    partial_value, log_total = attend(flat_rows, key_rows, value_rows, None)
    partial_value = partial_value.reshape(ctx_size, item_count, QG, head_count, HD)
    log_total = log_total.reshape(ctx_size, item_count, QG, head_count)
    partial_value, log_total = (partial_value, log_total)
    arrived = lax.all_to_all(
        partial_value.astype(jnp.float32), "ctx", split_axis=0, concat_axis=0, tiled=True
    ).astype(partial_value.dtype)
    arrived_log = lax.all_to_all(log_total, "ctx", split_axis=0, concat_axis=0, tiled=True)
    remote = jnp.take(arrived.reshape(slot_total, -1), slot_of, axis=0)
    remote_log = jnp.take(arrived_log.reshape(slot_total, -1), slot_of, axis=0)
    positions = jnp.arange(block_len, dtype=jnp.int32)
    visible = positions[:, None] >= positions[None, :]
    own_part, own_log = attend(
        query_rows,
        new_keys.reshape(block_len, head_count, HD),
        new_values.reshape(block_len, head_count, HD),
        visible,
    )
    remote = remote.reshape(groups, TOPK, QG, head_count, HD)
    remote_log = remote_log.reshape(groups, TOPK, QG, head_count)
    partials = jnp.concatenate([own_part.reshape(groups, 1, QG, head_count, HD), remote], axis=1)
    log_totals = jnp.concatenate([own_log.reshape(groups, 1, QG, head_count), remote_log], axis=1)
    top_log = jnp.max(log_totals, axis=1, keepdims=True)
    weights = jnp.exp(log_totals - top_log)
    row_total = jnp.sum(weights, axis=1)
    merged = (
        jnp.sum(weights[..., None] * partials.astype(jnp.float32), axis=1) / row_total[..., None]
    )
    merged = merged.astype(jnp.bfloat16).reshape(block_len, head_count * HD)
    return merged


def on_device(queries, cache_keys, cache_values, new_keys, new_values, chosen, out_weight):
    in_lines = lax.axis_size("ctx") == 8 and chosen.size * QG == 4 * queries.shape[0]
    attended = attention if in_lines else exchanged_attention
    merged = attended(queries, cache_keys, cache_values, new_keys, new_values, chosen)
    return project(merged, out_weight)


def solution(mesh):
    placed = (
        P("ctx", "head"),
        P("ctx", "head"),
        P("ctx", "head"),
        P("ctx", "head"),
        P("ctx", "head"),
        P("ctx", None),
        P("head", None),
    )
    return jax.shard_map(
        on_device, mesh=mesh, in_specs=placed, out_specs=P("ctx", "head"), check_vma=False
    )
```

```python
import functools
import math

import jax
import jax.numpy as jnp
from jax import lax
from jax.experimental import pallas as pl
from jax.experimental.pallas import tpu as pltpu
from jax.sharding import PartitionSpec as P

HD = 128
QG = 64
TOPK = 4
MESH = pl.DeviceIdType.MESH


def project_kernel(
    n_y, a_ref, w_ref, out_ref, w_buf, pair_out, pair_in, held, far_out, far_in,
    w_sem, pair_send, pair_recv, far_send, far_recv,
):
    head = lax.axis_index("head")
    core = lax.rem(head, 2)
    row = head // 2
    partner = head + 1 - 2 * core
    steps, _, tile = held.shape
    tiles = steps // n_y
    far = (n_y - 1) * tiles
    share = tiles * tile

    def w_copy(step, which):
        to_row = lax.rem(row + 1 + step // tiles, n_y)
        to_core = core if which else 1 - core
        start = (to_row * 2 + to_core) * share + lax.rem(step, tiles) * tile
        return pltpu.make_async_copy(
            w_ref.at[:, pl.ds(pl.multiple_of(start, tile), tile)],
            w_buf.at[which, step],
            w_sem.at[which, step],
        )

    def pair_copy(step):
        return pltpu.make_async_remote_copy(
            src_ref=pair_out.at[step], dst_ref=pair_in.at[step],
            send_sem=pair_send.at[step], recv_sem=pair_recv.at[step],
            device_id={"head": partner}, device_id_type=MESH,
        )

    def far_copy(step):
        to_row = lax.rem(row + 1 + step // tiles, n_y)
        return pltpu.make_async_remote_copy(
            src_ref=far_out.at[step], dst_ref=far_in.at[step],
            send_sem=far_send.at[step], recv_sem=far_recv.at[step],
            device_id={"head": to_row * 2 + core}, device_id_type=MESH,
        )

    @pl.loop(0, steps)
    def _(step):
        w_copy(step, 0).start()
        w_copy(step, 1).start()

    barrier = pltpu.get_barrier_semaphore()
    pl.semaphore_signal(barrier, inc=1, device_id={"head": partner}, device_id_type=MESH)
    for k in range(1, n_y):
        pl.semaphore_signal(
            barrier, inc=1, device_id={"head": lax.rem(row + k, n_y) * 2 + core},
            device_id_type=MESH,
        )
    pl.semaphore_wait(barrier, n_y)

    def finish(step):
        pair_copy(step).wait_recv()
        far_out[step] = (held[step] + pair_in[step].astype(jnp.float32)).astype(far_out.dtype)
        far_copy(step).start()

    @pl.loop(0, steps)
    def _(step):
        w_copy(step, 0).wait()
        pair_out[step] = jnp.dot(
            a_ref[...], w_buf[0, step], preferred_element_type=jnp.float32
        ).astype(pair_out.dtype)
        pair_copy(step).start()
        w_copy(step, 1).wait()
        held[step] = jnp.dot(a_ref[...], w_buf[1, step], preferred_element_type=jnp.float32)

        @pl.when((step >= 1) & (step <= far))
        def _():
            finish(step - 1)

    for j in range(tiles):
        pair_copy(far + j).wait_recv()
        total = held[far + j] + pair_in[far + j].astype(jnp.float32)
        for k in range(n_y - 1):
            far_copy(k * tiles + j).wait_recv()
            total = total + far_in[k * tiles + j].astype(jnp.float32)
        out_ref[:, j * tile : (j + 1) * tile] = total.astype(out_ref.dtype)

    @pl.loop(0, steps)
    def _(step):
        pair_copy(step).wait_send()

    @pl.loop(0, far)
    def _(step):
        far_copy(step).wait_send()


def project(merged, out_weight):
    rows, depth = merged.shape
    width = out_weight.shape[1]
    n_head = lax.axis_size("head")
    n_y = n_head // 2
    share = width // n_head
    tile = min(512, share)
    tiles = share // tile
    steps = n_y * tiles
    far = (n_y - 1) * tiles
    bf16 = jnp.bfloat16
    dma = pltpu.SemaphoreType.DMA
    return pl.pallas_call(
        functools.partial(project_kernel, n_y),
        out_shape=jax.ShapeDtypeStruct((rows, share), bf16),
        in_specs=[
            pl.BlockSpec(memory_space=pltpu.VMEM),
            pl.BlockSpec(memory_space=pl.ANY),
        ],
        out_specs=pl.BlockSpec(memory_space=pltpu.VMEM),
        scratch_shapes=[
            pltpu.VMEM((2, steps, depth, tile), bf16),
            pltpu.VMEM((steps, rows, tile), bf16),
            pltpu.VMEM((steps, rows, tile), bf16),
            pltpu.VMEM((steps, rows, tile), jnp.float32),
            pltpu.VMEM((far, rows, tile), bf16),
            pltpu.VMEM((far, rows, tile), bf16),
            dma((2, steps)), dma((steps,)), dma((steps,)), dma((far,)), dma((far,)),
        ],
        compiler_params=pltpu.CompilerParams(
            collective_id=1, has_side_effects=True, vmem_limit_bytes=56 * 1024 * 1024
        ),
        cost_estimate=pl.CostEstimate(
            flops=2 * rows * depth * width, bytes_accessed=2 * depth * width, transcendentals=0
        ),
    )(merged, out_weight)


def pack_kernel(q_ref, chosen_ref, pack_ref, spread_ref):
    groups = chosen_ref.shape[0]
    chunks, slot_rows, width = pack_ref.shape[2:]
    rows = q_ref.shape[0]
    slots = slot_rows // QG
    me = lax.axis_index("ctx")
    z, x = me // 2, lax.rem(me, 2)
    half = z // 2
    z_of = (1 + half, 3 * half, 2 - half, 3 - 3 * half)
    row_at = lax.broadcasted_iota(jnp.int32, (QG, rows), 0)
    col_at = lax.broadcasted_iota(jnp.int32, (QG, rows), 1)
    for col in range(2):
        for r in range(4):
            block = z_of[r] * 2 + (x if col == 0 else 1 - x)
            found = [jnp.int32(-1)] * slots
            count = jnp.int32(0)
            for g in range(groups):
                hit = jnp.int32(0)
                for k in range(TOPK):
                    hit = hit + (chosen_ref[g, k] == block).astype(jnp.int32)
                for s in range(slots):
                    found[s] = jnp.where((hit > 0) & (count == s), g, found[s])
                count = count + hit
            for s in range(slots):
                at = slice(s * QG, (s + 1) * QG)
                start = pl.multiple_of(jnp.maximum(found[s], 0) * QG, QG)
                for c in range(chunks):
                    pack_ref[col, r, c, at, :] = q_ref[
                        pl.ds(start, QG), c * width : (c + 1) * width
                    ]
                spread_ref[col, r, at, :] = jnp.where(
                    (col_at == row_at + start) & (found[s] >= 0), 1.0, 0.0
                ).astype(jnp.bfloat16)


def attention_kernel(
    q_ref, key_ref, value_ref, new_key_ref, new_value_ref, q_pack, spreads, merged_ref,
    keys, values, q_side, q_end, o_side, o_end, o_home, l_side, l_end, l_home,
    own_o, own_l, shares,
    load_sem, kv_send, kv_recv, q_send, side_q_recv, end_q_recv,
    side_o_send, end_o_send, o_recv, side_l_send, end_l_send, l_recv,
):
    chunks, _, width = keys.shape[1:]
    slot_rows = q_pack.shape[3]
    rows = q_ref.shape[0]
    per_chunk = width // HD
    scale = 1.0 / math.sqrt(HD)

    me = lax.axis_index("ctx")
    z, x = me // 2, lax.rem(me, 2)
    half = z // 2
    z_of = (1 + half, 3 * half, 2 - half, 3 - 3 * half)
    is_mid = (z == 1) | (z == 2)
    is_end = (z == 0) | (z == 3)
    own = jnp.where(is_mid, 0, 1)
    side = z * 2 + 1 - x
    pair_z = z_of[0] + z_of[1] - z
    pair, pair_across = pair_z * 2 + x, pair_z * 2 + 1 - x
    beyond = z_of[2] * 2 + x

    def remote(src, dst, send_sem, recv_sem, to):
        return pltpu.make_async_remote_copy(
            src_ref=src, dst_ref=dst, send_sem=send_sem, recv_sem=recv_sem,
            device_id={"ctx": to}, device_id_type=MESH,
        )

    def load(c, which):
        ref, held = ((key_ref, keys), (value_ref, values))[which]
        return pltpu.make_async_copy(
            ref.at[:, pl.ds(pl.multiple_of(c * width, width), width)],
            held.at[own, c], load_sem.at[c, which],
        )

    def kv_copy(kind, c, which):
        held = (keys, values)[which]
        src = 1 if kind == 2 else own
        dst = (own, 2, 3)[kind]
        return remote(
            held.at[src, c], held.at[dst, c], kv_send.at[kind, c, which],
            kv_recv.at[dst, c, which], pair if kind == 0 else beyond,
        )

    def side_q(r, c):
        return remote(
            q_pack.at[1, r, c], q_side.at[r, c], q_send.at[1, r, c], side_q_recv.at[r, c], side
        )

    def end_q(col, r, c):
        src = q_side if col else q_pack.at[0]
        return remote(
            src.at[r, c], q_end.at[col, r - 2, c], q_send.at[2 * col, r, c],
            end_q_recv.at[col, r - 2, c], pair,
        )

    def side_o(r, c):
        return remote(
            o_side.at[r, c], o_home.at[1, r, c], side_o_send.at[r, c], o_recv.at[1, r, c], side
        )

    def side_l(r):
        return remote(l_side.at[r], l_home.at[1, r], side_l_send.at[r], l_recv.at[1, r], side)

    def end_o(col, r, c):
        return remote(
            o_end.at[col, r - 2, c], o_home.at[col, r, c], end_o_send.at[col, r - 2, c],
            o_recv.at[col, r, c], (pair, pair_across)[col],
        )

    def end_l(col, r):
        return remote(
            l_end.at[col, r - 2], l_home.at[col, r], end_l_send.at[col, r - 2],
            l_recv.at[col, r], (pair, pair_across)[col],
        )

    for c in range(chunks):
        load(c, 0).start()
        load(c, 1).start()

    barrier = pltpu.get_barrier_semaphore()
    for to in (side, pair, pair_across):
        pl.semaphore_signal(barrier, inc=1, device_id={"ctx": to}, device_id_type=MESH)

    @pl.when(is_mid)
    def _():
        pl.semaphore_signal(barrier, inc=1, device_id={"ctx": beyond}, device_id_type=MESH)

    @pl.when(is_mid)
    def _():
        pl.semaphore_wait(barrier, 4)

    @pl.when(is_end)
    def _():
        pl.semaphore_wait(barrier, 3)

    def send_own(c):
        for which in range(2):
            load(c, which).wait()
            kv_copy(0, c, which).start()

    def send_end_q(col, r):
        @pl.loop(0, chunks)
        def _(c):
            if col:
                side_q(r, c).wait_recv()
            end_q(col, r, c).start()

    def send_side_q(r):
        @pl.loop(0, chunks)
        def _(c):
            side_q(r, c).start()

    @pl.when(is_mid)
    def _():
        send_side_q(0)

        @pl.loop(0, chunks)
        def _(c):
            send_own(c)
            for which in range(2):
                kv_copy(1, c, which).start()

        send_side_q(2)
        send_side_q(1)
        send_side_q(3)

    @pl.when(is_end)
    def _():
        send_side_q(2)
        send_side_q(3)
        for c in range(chunks // 2):
            send_own(c)
        send_end_q(0, 2)
        send_side_q(1)
        send_side_q(0)
        send_end_q(1, 2)
        for c in range(chunks // 2, chunks):
            send_own(c)
        send_end_q(0, 3)
        send_end_q(1, 3)

    def attend_one(q, k, v, first):
        scores = lax.dot_general(
            k, q, (((1,), (1,)), ((), ())), preferred_element_type=jnp.float32
        )
        if first is not None:
            key_at = lax.broadcasted_iota(jnp.int32, scores.shape, 0)
            query_at = lax.broadcasted_iota(jnp.int32, scores.shape, 1) + first
            scores = jnp.where(key_at <= query_at, scores, jnp.float32(-1e30))
        top = jnp.max(scores, axis=0, keepdims=True)
        weights = jnp.exp((scores - top) * scale)
        total = jnp.sum(weights, axis=0, keepdims=True)
        out = lax.dot_general(
            v, weights.astype(jnp.bfloat16), (((0,), (0,)), ((), ())),
            preferred_element_type=jnp.float32,
        )
        return (out * (1.0 / total)).astype(jnp.bfloat16), top * scale + jnp.log(total)

    def unit_pair(q_a, q_b, r, c, o_a, o_b, l_a, l_b):
        for i in range(per_chunk):
            at = slice(i * HD, (i + 1) * HD)
            q = jnp.concatenate([q_a[:, at], q_b[:, at]], axis=0)
            out, log = attend_one(q, keys[r, c, :, at], values[r, c, :, at], None)
            row = pl.ds(c * per_chunk + i, 1)
            for n, (o_dst, l_dst) in enumerate(((o_a, l_a), (o_b, l_b))):
                half_at = slice(n * slot_rows, (n + 1) * slot_rows)
                o_dst[at, :] = out[:, half_at]
                l_dst[row, :] = log[:, half_at]

    @pl.loop(0, chunks * per_chunk)
    def _(h):
        cols = pl.ds(pl.multiple_of(h * HD, HD), HD)
        for first in range(0, rows, slot_rows):
            seen = first + slot_rows
            out, log = attend_one(
                q_ref[first:seen, cols], new_key_ref[:seen, cols], new_value_ref[:seen, cols], first
            )
            own_o[h, :, first:seen] = out
            own_l[pl.ds(h, 1), first:seen] = log

    def work(r, c):
        @pl.when(r != own)
        def _():
            for which in range(2):
                held = (keys, values)[which].at[r, c]
                remote(held, held, kv_send.at[0, c, which], kv_recv.at[r, c, which], pair).wait_recv()

        @pl.when(is_mid & (r == 1))
        def _():
            for which in range(2):
                kv_copy(2, c, which).start()

        side_q(r, c).wait_recv()
        unit_pair(
            q_pack.at[0, r, c], q_side.at[r, c], r, c,
            o_home.at[0, r, c], o_side.at[r, c], l_home.at[0, r], l_side.at[r],
        )
        side_o(r, c).start()

        @pl.when(c == chunks - 1)
        def _():
            side_l(r).start()

        @pl.when(r >= 2)
        def _():
            for col in range(2):
                end_q(col, r, c).wait_recv()
            unit_pair(
                q_end.at[0, r - 2, c], q_end.at[1, r - 2, c], r, c,
                o_end.at[0, r - 2, c], o_end.at[1, r - 2, c], l_end.at[0, r - 2], l_end.at[1, r - 2],
            )
            for col in range(2):
                end_o(col, r, c).start()

            @pl.when(c == chunks - 1)
            def _():
                for col in range(2):
                    end_l(col, r).start()

    ahead = min(chunks, chunks // 2 + 1)

    @pl.loop(0, jnp.where(is_mid, 4, 2) * chunks)
    def _(step):
        late = step - 2 * chunks - ahead
        lead = late < 0
        even = lax.rem(late, 2) == 0
        near_end = lead | ((late < 2 * (chunks - ahead)) & jnp.logical_not(even))
        near_c = jnp.where(lead, step - 2 * chunks, ahead + late // 2)
        far_c = jnp.where(late < 2 * (chunks - ahead), late // 2, late - (chunks - ahead))
        first = step < chunks
        second = (step >= chunks) & (step < 2 * chunks)
        r = jnp.where(
            first, own,
            jnp.where(second, jnp.where(is_mid, 2, 1 - own), jnp.where(near_end, 1, 3)),
        )
        c = jnp.where(
            first | second, lax.rem(step, chunks), jnp.where(near_end, near_c, far_c)
        )
        work(r, c)

    @pl.loop(0, 4)
    def _(r):
        side_l(r).wait_recv()

        @pl.loop(0, chunks)
        def _(c):
            side_o(r, c).wait_recv()

    @pl.when(is_end)
    def _():
        @pl.loop(2, 4)
        def _(r):
            end_l(0, r).wait_recv()

            @pl.loop(0, chunks)
            def _(c):
                end_o(0, r, c).wait_recv()

    logs = []
    for n in range(8):
        placed = spreads[n // 4, n % 4]
        rest = l_home[n // 4, n % 4]
        log = jnp.zeros((rest.shape[0], rows), jnp.float32)
        for _ in range(3):
            piece = rest.astype(jnp.bfloat16)
            rest = rest - piece.astype(jnp.float32)
            log = log + jnp.dot(piece, placed, preferred_element_type=jnp.float32)
        hit = jnp.sum(placed.astype(jnp.float32), axis=0, keepdims=True)
        logs.append(jnp.where(hit > 0, log, jnp.float32(-1e30)))
    logs.append(own_l[...])
    top = functools.reduce(jnp.maximum, logs)
    weights = [jnp.exp(log - top) for log in logs]
    inverse = 1.0 / functools.reduce(jnp.add, weights)
    for n, weight in enumerate(weights):
        shares[n] = weight * inverse

    for c in range(chunks):
        heads = range(c * per_chunk, (c + 1) * per_chunk)
        total = [own_o[h].astype(jnp.float32) * shares[8, h : h + 1, :] for h in heads]
        for n in range(8):
            part = jnp.dot(
                o_home[n // 4, n % 4, c], spreads[n // 4, n % 4],
                preferred_element_type=jnp.float32,
            )
            for i, h in enumerate(heads):
                total[i] = total[i] + part[i * HD : (i + 1) * HD] * shares[n, h : h + 1, :]
        for i, h in enumerate(heads):
            merged_ref[:, h * HD : (h + 1) * HD] = total[i].T.astype(merged_ref.dtype)

    @pl.loop(0, chunks)
    def _(c):
        for which in range(2):
            kv_copy(0, c, which).wait_send()

        @pl.loop(0, 4)
        def _(r):
            side_q(r, c).wait_send()

        @pl.loop(0, 2)
        def _(r):
            side_o(r, c).wait_send()

        @pl.when(is_mid)
        def _():
            for which in range(2):
                kv_copy(1, c, which).wait_send()
                kv_copy(2, c, which).wait_send()

            @pl.loop(2, 4)
            def _(r):
                side_o(r, c).wait_send()
                for col in range(2):
                    end_o(col, r, c).wait_send()

        @pl.when(is_end)
        def _():
            @pl.loop(2, 4)
            def _(r):
                for col in range(2):
                    end_q(col, r, c).wait_send()

    @pl.loop(0, 2)
    def _(r):
        side_l(r).wait_send()

    @pl.when(is_mid)
    def _():
        @pl.loop(2, 4)
        def _(r):
            side_l(r).wait_send()
            for col in range(2):
                end_l(col, r).wait_send()


def attention(queries, cache_keys, cache_values, new_keys, new_values, chosen):
    rows, columns = queries.shape
    heads = columns // HD
    width = min(2 * HD, columns)
    chunks = columns // width
    slot_rows = chosen.size // lax.axis_size("ctx") * QG
    bf16, f32 = jnp.bfloat16, jnp.float32
    dma = pltpu.SemaphoreType.DMA
    in_vmem = pl.BlockSpec(memory_space=pltpu.VMEM)
    in_hbm = pl.BlockSpec(memory_space=pl.ANY)
    work = (slot_rows * 8 + rows) * rows * columns
    packed, spreads = pl.pallas_call(
        pack_kernel,
        out_shape=(
            jax.ShapeDtypeStruct((2, 4, chunks, slot_rows, width), bf16),
            jax.ShapeDtypeStruct((2, 4, slot_rows, rows), bf16),
        ),
        in_specs=[in_vmem, pl.BlockSpec(memory_space=pltpu.SMEM)],
        out_specs=(in_vmem, in_vmem),
        compiler_params=pltpu.CompilerParams(vmem_limit_bytes=24 * 1024 * 1024),
    )(queries, chosen)
    return pl.pallas_call(
        attention_kernel,
        out_shape=jax.ShapeDtypeStruct((rows, columns), bf16),
        in_specs=[
            in_vmem, in_hbm, in_hbm, in_vmem, in_vmem, in_vmem, in_vmem
        ],
        out_specs=in_vmem,
        scratch_shapes=[
            pltpu.VMEM((4, chunks, rows, width), bf16),
            pltpu.VMEM((4, chunks, rows, width), bf16),
            pltpu.VMEM((4, chunks, slot_rows, width), bf16),
            pltpu.VMEM((2, 2, chunks, slot_rows, width), bf16),
            pltpu.VMEM((4, chunks, width, slot_rows), bf16),
            pltpu.VMEM((2, 2, chunks, width, slot_rows), bf16),
            pltpu.VMEM((2, 4, chunks, width, slot_rows), bf16),
            pltpu.VMEM((4, heads, slot_rows), f32),
            pltpu.VMEM((2, 2, heads, slot_rows), f32),
            pltpu.VMEM((2, 4, heads, slot_rows), f32),
            pltpu.VMEM((heads, HD, rows), bf16),
            pltpu.VMEM((heads, rows), f32),
            pltpu.VMEM((9, heads, rows), f32),
            dma((chunks, 2)), dma((3, chunks, 2)), dma((4, chunks, 2)), dma((3, 4, chunks)),
            dma((4, chunks)), dma((2, 2, chunks)),
            dma((4, chunks)), dma((2, 2, chunks)), dma((2, 4, chunks)),
            dma((4,)), dma((2, 2)), dma((2, 4)),
        ],
        compiler_params=pltpu.CompilerParams(
            collective_id=0, has_side_effects=True, vmem_limit_bytes=56 * 1024 * 1024
        ),
        cost_estimate=pl.CostEstimate(
            flops=4 * work, bytes_accessed=12 * rows * columns, transcendentals=work // HD
        ),
    )(queries, cache_keys, cache_values, new_keys, new_values, packed, spreads)


def attend(query_rows, key_rows, value_rows, visible):
    partials = []
    log_totals = []
    for head_number in range(query_rows.shape[1]):
        scores = lax.dot_general(
            query_rows[:, head_number],
            key_rows[:, head_number],
            (((1,), (1,)), ((), ())),
            preferred_element_type=jnp.float32,
        ) / math.sqrt(HD)
        if visible is not None:
            scores = jnp.where(visible, scores, jnp.float32(-1e30))
        row_max = jnp.max(scores, axis=-1, keepdims=True)
        weights = jnp.exp(scores - row_max)
        row_total = jnp.sum(weights, axis=-1, keepdims=True)
        probs = (weights / row_total).astype(jnp.bfloat16)
        partial_value = jnp.dot(
            probs, value_rows[:, head_number], preferred_element_type=jnp.float32
        )
        partials.append(partial_value.astype(jnp.bfloat16))
        log_totals.append((row_max + jnp.log(row_total))[:, 0])
    return (jnp.stack(partials, axis=1), jnp.stack(log_totals, axis=1))


def pack_slots(queries, slot_index, live, slot_total, groups, ctx_size, capacity, head_count):
    pair_total = slot_index.shape[0]
    slot_pick = (
        (jnp.arange(slot_total, dtype=jnp.int32)[:, None] == slot_index[None, :]) & live[None, :]
    ).astype(jnp.bfloat16)
    pair_group = jnp.arange(pair_total, dtype=jnp.int32) // TOPK
    group_pick = (pair_group[:, None] == jnp.arange(groups, dtype=jnp.int32)[None, :]).astype(
        jnp.bfloat16
    )
    slot_group = jnp.dot(slot_pick, group_pick, preferred_element_type=jnp.float32).astype(
        jnp.bfloat16
    )
    outgoing = jnp.dot(slot_group, queries.reshape(groups, -1), preferred_element_type=jnp.float32)
    return outgoing.astype(jnp.bfloat16).reshape(ctx_size, capacity, QG, head_count, HD)


def exchanged_attention(queries, cache_keys, cache_values, new_keys, new_values, chosen):
    block_len = queries.shape[0]
    head_count = queries.shape[1] // HD
    groups = block_len // QG
    ctx_size = lax.axis_size("ctx")
    capacity = max(2, (groups * TOPK + ctx_size - 1) // ctx_size)
    query_rows = queries.reshape(block_len, head_count, HD)
    key_rows = cache_keys.reshape(block_len, head_count, HD)
    value_rows = cache_values.reshape(block_len, head_count, HD)
    target = chosen.reshape(-1)
    pair_total = target.shape[0]
    target_hit = (target[:, None] == jnp.arange(ctx_size, dtype=jnp.int32)[None, :]).astype(
        jnp.int32
    )
    before = jnp.sum((jnp.cumsum(target_hit, axis=0) - target_hit) * target_hit, axis=1)
    every_pair = jnp.ones((pair_total,), bool)
    slot_total = ctx_size * capacity
    slot_of = target * capacity + before
    outgoing = pack_slots(
        queries, slot_of, every_pair, slot_total, groups, ctx_size, capacity, head_count
    )
    incoming = lax.all_to_all(outgoing, "ctx", split_axis=0, concat_axis=0, tiled=True)
    item_count = incoming.shape[1]
    flat_rows = incoming.reshape(-1, head_count, HD)
    partial_value, log_total = attend(flat_rows, key_rows, value_rows, None)
    partial_value = partial_value.reshape(ctx_size, item_count, QG, head_count, HD)
    log_total = log_total.reshape(ctx_size, item_count, QG, head_count)
    partial_value, log_total = (partial_value, log_total)
    arrived = lax.all_to_all(
        partial_value.astype(jnp.float32), "ctx", split_axis=0, concat_axis=0, tiled=True
    ).astype(partial_value.dtype)
    arrived_log = lax.all_to_all(log_total, "ctx", split_axis=0, concat_axis=0, tiled=True)
    remote = jnp.take(arrived.reshape(slot_total, -1), slot_of, axis=0)
    remote_log = jnp.take(arrived_log.reshape(slot_total, -1), slot_of, axis=0)
    positions = jnp.arange(block_len, dtype=jnp.int32)
    visible = positions[:, None] >= positions[None, :]
    own_part, own_log = attend(
        query_rows,
        new_keys.reshape(block_len, head_count, HD),
        new_values.reshape(block_len, head_count, HD),
        visible,
    )
    remote = remote.reshape(groups, TOPK, QG, head_count, HD)
    remote_log = remote_log.reshape(groups, TOPK, QG, head_count)
    partials = jnp.concatenate([own_part.reshape(groups, 1, QG, head_count, HD), remote], axis=1)
    log_totals = jnp.concatenate([own_log.reshape(groups, 1, QG, head_count), remote_log], axis=1)
    top_log = jnp.max(log_totals, axis=1, keepdims=True)
    weights = jnp.exp(log_totals - top_log)
    row_total = jnp.sum(weights, axis=1)
    merged = (
        jnp.sum(weights[..., None] * partials.astype(jnp.float32), axis=1) / row_total[..., None]
    )
    merged = merged.astype(jnp.bfloat16).reshape(block_len, head_count * HD)
    return merged


def on_device(queries, cache_keys, cache_values, new_keys, new_values, chosen, out_weight):
    in_lines = lax.axis_size("ctx") == 8 and chosen.size * QG == 4 * queries.shape[0]
    attended = attention if in_lines else exchanged_attention
    merged = attended(queries, cache_keys, cache_values, new_keys, new_values, chosen)
    return project(merged, out_weight)


def solution(mesh):
    placed = (
        P("ctx", "head"),
        P("ctx", "head"),
        P("ctx", "head"),
        P("ctx", "head"),
        P("ctx", "head"),
        P("ctx", None),
        P("head", None),
    )
    return jax.shard_map(
        on_device, mesh=mesh, in_specs=placed, out_specs=P("ctx", "head"), check_vma=False
    )
```

```python
import functools
import math

import jax
import jax.numpy as jnp
from jax import lax
from jax.experimental import pallas as pl
from jax.experimental.pallas import tpu as pltpu
from jax.sharding import PartitionSpec as P

HD = 128
QG = 64
TOPK = 4
MESH = pl.DeviceIdType.MESH


def project_kernel(
    n_y, a_ref, w_ref, out_ref, w_buf, pair_out, pair_in, held, far_out, far_in,
    w_sem, pair_send, pair_recv, far_send, far_recv,
):
    head = lax.axis_index("head")
    core = lax.rem(head, 2)
    row = head // 2
    partner = head + 1 - 2 * core
    steps, _, tile = held.shape
    tiles = steps // n_y
    far = (n_y - 1) * tiles
    share = tiles * tile

    def w_copy(step, which):
        to_row = lax.rem(row + 1 + step // tiles, n_y)
        to_core = core if which else 1 - core
        start = (to_row * 2 + to_core) * share + lax.rem(step, tiles) * tile
        return pltpu.make_async_copy(
            w_ref.at[:, pl.ds(pl.multiple_of(start, tile), tile)],
            w_buf.at[which, step],
            w_sem.at[which, step],
        )

    def pair_copy(step):
        return pltpu.make_async_remote_copy(
            src_ref=pair_out.at[step], dst_ref=pair_in.at[step],
            send_sem=pair_send.at[step], recv_sem=pair_recv.at[step],
            device_id={"head": partner}, device_id_type=MESH,
        )

    def far_copy(step):
        to_row = lax.rem(row + 1 + step // tiles, n_y)
        return pltpu.make_async_remote_copy(
            src_ref=far_out.at[step], dst_ref=far_in.at[step],
            send_sem=far_send.at[step], recv_sem=far_recv.at[step],
            device_id={"head": to_row * 2 + core}, device_id_type=MESH,
        )

    @pl.loop(0, steps)
    def _(step):
        w_copy(step, 0).start()
        w_copy(step, 1).start()

    barrier = pltpu.get_barrier_semaphore()
    pl.semaphore_signal(barrier, inc=1, device_id={"head": partner}, device_id_type=MESH)
    for k in range(1, n_y):
        pl.semaphore_signal(
            barrier, inc=1, device_id={"head": lax.rem(row + k, n_y) * 2 + core},
            device_id_type=MESH,
        )
    pl.semaphore_wait(barrier, n_y)

    def finish(step):
        pair_copy(step).wait_recv()
        far_out[step] = (held[step] + pair_in[step].astype(jnp.float32)).astype(far_out.dtype)
        far_copy(step).start()

    @pl.loop(0, steps)
    def _(step):
        w_copy(step, 0).wait()
        pair_out[step] = jnp.dot(
            a_ref[...], w_buf[0, step], preferred_element_type=jnp.float32
        ).astype(pair_out.dtype)
        pair_copy(step).start()
        w_copy(step, 1).wait()
        held[step] = jnp.dot(a_ref[...], w_buf[1, step], preferred_element_type=jnp.float32)

        @pl.when((step >= 1) & (step <= far))
        def _():
            finish(step - 1)

    for j in range(tiles):
        pair_copy(far + j).wait_recv()
        total = held[far + j] + pair_in[far + j].astype(jnp.float32)
        for k in range(n_y - 1):
            far_copy(k * tiles + j).wait_recv()
            total = total + far_in[k * tiles + j].astype(jnp.float32)
        out_ref[:, j * tile : (j + 1) * tile] = total.astype(out_ref.dtype)

    @pl.loop(0, steps)
    def _(step):
        pair_copy(step).wait_send()

    @pl.loop(0, far)
    def _(step):
        far_copy(step).wait_send()


def project(merged, out_weight):
    rows, depth = merged.shape
    width = out_weight.shape[1]
    n_head = lax.axis_size("head")
    n_y = n_head // 2
    share = width // n_head
    tile = min(512, share)
    tiles = share // tile
    steps = n_y * tiles
    far = (n_y - 1) * tiles
    bf16 = jnp.bfloat16
    dma = pltpu.SemaphoreType.DMA
    return pl.pallas_call(
        functools.partial(project_kernel, n_y),
        out_shape=jax.ShapeDtypeStruct((rows, share), bf16),
        in_specs=[
            pl.BlockSpec(memory_space=pltpu.VMEM),
            pl.BlockSpec(memory_space=pl.ANY),
        ],
        out_specs=pl.BlockSpec(memory_space=pltpu.VMEM),
        scratch_shapes=[
            pltpu.VMEM((2, steps, depth, tile), bf16),
            pltpu.VMEM((steps, rows, tile), bf16),
            pltpu.VMEM((steps, rows, tile), bf16),
            pltpu.VMEM((steps, rows, tile), jnp.float32),
            pltpu.VMEM((far, rows, tile), bf16),
            pltpu.VMEM((far, rows, tile), bf16),
            dma((2, steps)), dma((steps,)), dma((steps,)), dma((far,)), dma((far,)),
        ],
        compiler_params=pltpu.CompilerParams(
            collective_id=1, has_side_effects=True, vmem_limit_bytes=56 * 1024 * 1024
        ),
        cost_estimate=pl.CostEstimate(
            flops=2 * rows * depth * width, bytes_accessed=2 * depth * width, transcendentals=0
        ),
    )(merged, out_weight)


def pack_kernel(q_ref, chosen_ref, pack_ref, spread_ref):
    groups = chosen_ref.shape[0]
    chunks, slot_rows, width = pack_ref.shape[2:]
    rows = q_ref.shape[0]
    slots = slot_rows // QG
    me = lax.axis_index("ctx")
    z, x = me // 2, lax.rem(me, 2)
    half = z // 2
    z_of = (1 + half, 3 * half, 2 - half, 3 - 3 * half)
    row_at = lax.broadcasted_iota(jnp.int32, (QG, rows), 0)
    col_at = lax.broadcasted_iota(jnp.int32, (QG, rows), 1)
    for col in range(2):
        for r in range(4):
            block = z_of[r] * 2 + (x if col == 0 else 1 - x)
            found = [jnp.int32(-1)] * slots
            count = jnp.int32(0)
            for g in range(groups):
                hit = jnp.int32(0)
                for k in range(TOPK):
                    hit = hit + (chosen_ref[g, k] == block).astype(jnp.int32)
                for s in range(slots):
                    found[s] = jnp.where((hit > 0) & (count == s), g, found[s])
                count = count + hit
            for s in range(slots):
                at = slice(s * QG, (s + 1) * QG)
                start = pl.multiple_of(jnp.maximum(found[s], 0) * QG, QG)
                for c in range(chunks):
                    pack_ref[col, r, c, at, :] = q_ref[
                        pl.ds(start, QG), c * width : (c + 1) * width
                    ]
                spread_ref[col, r, at, :] = jnp.where(
                    (col_at == row_at + start) & (found[s] >= 0), 1.0, 0.0
                ).astype(jnp.bfloat16)


def attention_kernel(
    q_ref, key_ref, value_ref, new_key_ref, new_value_ref, q_pack, spreads, merged_ref,
    keys, values, q_side, q_end, o_side, o_end, o_home, l_side, l_end, l_home,
    own_o, own_l,
    load_sem, kv_send, kv_recv, q_send, side_q_recv, end_q_recv,
    side_o_send, end_o_send, o_recv, side_l_send, end_l_send, l_recv,
):
    chunks, _, width = keys.shape[1:]
    slot_rows = q_pack.shape[3]
    rows = q_ref.shape[0]
    per_chunk = width // HD
    scale = 1.0 / math.sqrt(HD)

    me = lax.axis_index("ctx")
    z, x = me // 2, lax.rem(me, 2)
    half = z // 2
    z_of = (1 + half, 3 * half, 2 - half, 3 - 3 * half)
    is_mid = (z == 1) | (z == 2)
    is_end = (z == 0) | (z == 3)
    own = jnp.where(is_mid, 0, 1)
    side = z * 2 + 1 - x
    pair_z = z_of[0] + z_of[1] - z
    pair, pair_across = pair_z * 2 + x, pair_z * 2 + 1 - x
    beyond = z_of[2] * 2 + x

    def remote(src, dst, send_sem, recv_sem, to):
        return pltpu.make_async_remote_copy(
            src_ref=src, dst_ref=dst, send_sem=send_sem, recv_sem=recv_sem,
            device_id={"ctx": to}, device_id_type=MESH,
        )

    def load(c, which):
        ref, held = ((key_ref, keys), (value_ref, values))[which]
        return pltpu.make_async_copy(
            ref.at[:, pl.ds(pl.multiple_of(c * width, width), width)],
            held.at[own, c], load_sem.at[c, which],
        )

    def kv_copy(kind, c, which):
        held = (keys, values)[which]
        src = 1 if kind == 2 else own
        dst = (own, 2, 3)[kind]
        return remote(
            held.at[src, c], held.at[dst, c], kv_send.at[kind, c, which],
            kv_recv.at[dst, c, which], pair if kind == 0 else beyond,
        )

    def side_q(r, c):
        return remote(
            q_pack.at[1, r, c], q_side.at[r, c], q_send.at[1, r, c], side_q_recv.at[r, c], side
        )

    def end_q(col, r, c):
        src = q_side if col else q_pack.at[0]
        return remote(
            src.at[r, c], q_end.at[col, r - 2, c], q_send.at[2 * col, r, c],
            end_q_recv.at[col, r - 2, c], pair,
        )

    def side_o(r, c):
        return remote(
            o_side.at[r, c], o_home.at[1, r, c], side_o_send.at[r, c], o_recv.at[1, r, c], side
        )

    def side_l(r, c):
        return remote(
            l_side.at[r, c], l_home.at[1, r, c], side_l_send.at[r, c], l_recv.at[1, r, c], side
        )

    def end_o(col, r, c):
        return remote(
            o_end.at[col, r - 2, c], o_home.at[col, r, c], end_o_send.at[col, r - 2, c],
            o_recv.at[col, r, c], (pair, pair_across)[col],
        )

    def end_l(col, r, c):
        return remote(
            l_end.at[col, r - 2, c], l_home.at[col, r, c], end_l_send.at[col, r - 2, c],
            l_recv.at[col, r, c], (pair, pair_across)[col],
        )

    for c in range(chunks):
        load(c, 0).start()
        load(c, 1).start()

    barrier = pltpu.get_barrier_semaphore()
    for to in (side, pair, pair_across):
        pl.semaphore_signal(barrier, inc=1, device_id={"ctx": to}, device_id_type=MESH)

    @pl.when(is_mid)
    def _():
        pl.semaphore_signal(barrier, inc=1, device_id={"ctx": beyond}, device_id_type=MESH)

    @pl.when(is_mid)
    def _():
        pl.semaphore_wait(barrier, 4)

    @pl.when(is_end)
    def _():
        pl.semaphore_wait(barrier, 3)

    def send_own(c):
        for which in range(2):
            load(c, which).wait()
            kv_copy(0, c, which).start()

    def send_end_q(col, r):
        @pl.loop(0, chunks)
        def _(c):
            if col:
                side_q(r, c).wait_recv()
            end_q(col, r, c).start()

    def send_side_q(r):
        @pl.loop(0, chunks)
        def _(c):
            side_q(r, c).start()

    @pl.when(is_mid)
    def _():
        send_side_q(0)

        @pl.loop(0, chunks)
        def _(c):
            send_own(c)
            for which in range(2):
                kv_copy(1, c, which).start()

        send_side_q(2)
        send_side_q(1)
        send_side_q(3)

    @pl.when(is_end)
    def _():
        send_side_q(2)
        send_side_q(3)
        for c in range(chunks // 2):
            send_own(c)
        send_end_q(0, 2)
        send_side_q(1)
        send_side_q(0)
        send_end_q(1, 2)
        for c in range(chunks // 2, chunks):
            send_own(c)
        send_end_q(0, 3)
        send_end_q(1, 3)

    def attend_one(q, k, v, first):
        scores = lax.dot_general(
            k, q, (((1,), (1,)), ((), ())), preferred_element_type=jnp.float32
        )
        if first is not None:
            key_at = lax.broadcasted_iota(jnp.int32, scores.shape, 0)
            query_at = lax.broadcasted_iota(jnp.int32, scores.shape, 1) + first
            scores = jnp.where(key_at <= query_at, scores, jnp.float32(-1e30))
        top = jnp.max(scores, axis=0, keepdims=True)
        weights = jnp.exp((scores - top) * scale)
        total = jnp.sum(weights, axis=0, keepdims=True)
        out = lax.dot_general(
            v, weights.astype(jnp.bfloat16), (((0,), (0,)), ((), ())),
            preferred_element_type=jnp.float32,
        )
        return (out * (1.0 / total)).astype(jnp.bfloat16), top * scale + jnp.log(total)

    def unit_pair(q_a, q_b, r, c, o_a, o_b, l_a, l_b):
        for i in range(per_chunk):
            at = slice(i * HD, (i + 1) * HD)
            q = jnp.concatenate([q_a[:, at], q_b[:, at]], axis=0)
            out, log = attend_one(q, keys[r, c, :, at], values[r, c, :, at], None)
            for n, (o_dst, l_dst) in enumerate(((o_a, l_a), (o_b, l_b))):
                half_at = slice(n * slot_rows, (n + 1) * slot_rows)
                o_dst[at, :] = out[:, half_at]
                l_dst[i : i + 1, :] = log[:, half_at]

    @pl.loop(0, chunks * per_chunk)
    def _(h):
        cols = pl.ds(pl.multiple_of(h * HD, HD), HD)
        for first in range(0, rows, slot_rows):
            seen = first + slot_rows
            out, log = attend_one(
                q_ref[first:seen, cols], new_key_ref[:seen, cols], new_value_ref[:seen, cols], first
            )
            own_o[h, :, first:seen] = out
            own_l[pl.ds(h, 1), first:seen] = log

    def arrived(r, c):
        for which in range(2):
            held = (keys, values)[which].at[r, c]
            remote(held, held, kv_send.at[0, c, which], kv_recv.at[r, c, which], pair).wait_recv()

    early = chunks // 2

    def work(r, c):
        @pl.when((r != own) & jnp.logical_not(is_mid & (r == 1)))
        def _():
            arrived(r, c)

        @pl.when(is_mid & (((r == 1) & (c >= early)) | ((r == 2) & (c < early))))
        def _():
            arrived(1, c)
            for which in range(2):
                kv_copy(2, c, which).start()

        @pl.when(r >= 2)
        def _():
            for col in range(2):
                end_q(col, r, c).wait_recv()
            unit_pair(
                q_end.at[0, r - 2, c], q_end.at[1, r - 2, c], r, c,
                o_end.at[0, r - 2, c], o_end.at[1, r - 2, c], l_end.at[0, r - 2, c], l_end.at[1, r - 2, c],
            )
            for col in range(2):
                end_o(col, r, c).start()
                end_l(col, r, c).start()

        side_q(r, c).wait_recv()
        unit_pair(
            q_pack.at[0, r, c], q_side.at[r, c], r, c,
            o_home.at[0, r, c], o_side.at[r, c], l_home.at[0, r, c], l_side.at[r, c],
        )
        side_o(r, c).start()
        side_l(r, c).start()

    ahead = min(chunks, chunks // 2 + 1)

    @pl.loop(0, jnp.where(is_mid, 4, 2) * chunks)
    def _(step):
        late = step - 2 * chunks - ahead
        lead = late < 0
        even = lax.rem(late, 2) == 0
        near_end = lead | ((late < 2 * (chunks - ahead)) & jnp.logical_not(even))
        near_c = jnp.where(lead, step - 2 * chunks, ahead + late // 2)
        far_c = jnp.where(late < 2 * (chunks - ahead), late // 2, late - (chunks - ahead))
        first = step < chunks
        second = (step >= chunks) & (step < 2 * chunks)
        r = jnp.where(
            first, own,
            jnp.where(second, jnp.where(is_mid, 2, 1 - own), jnp.where(near_end, 1, 3)),
        )
        c = jnp.where(
            first | second, lax.rem(step, chunks), jnp.where(near_end, near_c, far_c)
        )
        work(r, c)

    def merge(c):
        @pl.loop(0, 4)
        def _(r):
            side_l(r, c).wait_recv()
            side_o(r, c).wait_recv()

        @pl.when(is_end)
        def _():
            for r in (2, 3):
                end_l(0, r, c).wait_recv()
                end_o(0, r, c).wait_recv()

        heads = range(c * per_chunk, (c + 1) * per_chunk)
        logs = []
        for n in range(8):
            placed = spreads[n // 4, n % 4]
            rest = l_home[n // 4, n % 4, c]
            log = jnp.zeros((per_chunk, rows), jnp.float32)
            for _ in range(3):
                piece = rest.astype(jnp.bfloat16)
                rest = rest - piece.astype(jnp.float32)
                log = log + jnp.dot(piece, placed, preferred_element_type=jnp.float32)
            hit = jnp.sum(placed.astype(jnp.float32), axis=0, keepdims=True)
            logs.append(jnp.where(hit > 0, log, jnp.float32(-1e30)))
        logs.append(own_l[heads[0] : heads[-1] + 1, :])
        top = functools.reduce(jnp.maximum, logs)
        weights = [jnp.exp(log - top) for log in logs]
        inverse = 1.0 / functools.reduce(jnp.add, weights)
        shares = [weight * inverse for weight in weights]
        total = [
            own_o[h].astype(jnp.float32) * shares[8][i : i + 1, :] for i, h in enumerate(heads)
        ]
        for n in range(8):
            part = jnp.dot(
                o_home[n // 4, n % 4, c], spreads[n // 4, n % 4],
                preferred_element_type=jnp.float32,
            )
            for i in range(per_chunk):
                total[i] = total[i] + part[i * HD : (i + 1) * HD] * shares[n][i : i + 1, :]
        for i, h in enumerate(heads):
            merged_ref[:, h * HD : (h + 1) * HD] = total[i].T.astype(merged_ref.dtype)

    for c in range(chunks):
        merge(c)

    @pl.loop(0, chunks)
    def _(c):
        for which in range(2):
            kv_copy(0, c, which).wait_send()

        @pl.loop(0, 4)
        def _(r):
            side_q(r, c).wait_send()

        @pl.loop(0, 2)
        def _(r):
            side_o(r, c).wait_send()
            side_l(r, c).wait_send()

        @pl.when(is_mid)
        def _():
            for which in range(2):
                kv_copy(1, c, which).wait_send()
                kv_copy(2, c, which).wait_send()

            @pl.loop(2, 4)
            def _(r):
                side_o(r, c).wait_send()
                side_l(r, c).wait_send()
                for col in range(2):
                    end_o(col, r, c).wait_send()
                    end_l(col, r, c).wait_send()

        @pl.when(is_end)
        def _():
            @pl.loop(2, 4)
            def _(r):
                for col in range(2):
                    end_q(col, r, c).wait_send()


def attention(queries, cache_keys, cache_values, new_keys, new_values, chosen):
    rows, columns = queries.shape
    heads = columns // HD
    width = min(2 * HD, columns)
    chunks = columns // width
    slot_rows = chosen.size // lax.axis_size("ctx") * QG
    bf16, f32 = jnp.bfloat16, jnp.float32
    dma = pltpu.SemaphoreType.DMA
    in_vmem = pl.BlockSpec(memory_space=pltpu.VMEM)
    in_hbm = pl.BlockSpec(memory_space=pl.ANY)
    work = (slot_rows * 8 + rows) * rows * columns
    packed, spreads = pl.pallas_call(
        pack_kernel,
        out_shape=(
            jax.ShapeDtypeStruct((2, 4, chunks, slot_rows, width), bf16),
            jax.ShapeDtypeStruct((2, 4, slot_rows, rows), bf16),
        ),
        in_specs=[in_vmem, pl.BlockSpec(memory_space=pltpu.SMEM)],
        out_specs=(in_vmem, in_vmem),
        compiler_params=pltpu.CompilerParams(vmem_limit_bytes=24 * 1024 * 1024),
    )(queries, chosen)
    return pl.pallas_call(
        attention_kernel,
        out_shape=jax.ShapeDtypeStruct((rows, columns), bf16),
        in_specs=[
            in_vmem, in_hbm, in_hbm, in_vmem, in_vmem, in_vmem, in_vmem
        ],
        out_specs=in_vmem,
        scratch_shapes=[
            pltpu.VMEM((4, chunks, rows, width), bf16),
            pltpu.VMEM((4, chunks, rows, width), bf16),
            pltpu.VMEM((4, chunks, slot_rows, width), bf16),
            pltpu.VMEM((2, 2, chunks, slot_rows, width), bf16),
            pltpu.VMEM((4, chunks, width, slot_rows), bf16),
            pltpu.VMEM((2, 2, chunks, width, slot_rows), bf16),
            pltpu.VMEM((2, 4, chunks, width, slot_rows), bf16),
            pltpu.VMEM((4, chunks, width // HD, slot_rows), f32),
            pltpu.VMEM((2, 2, chunks, width // HD, slot_rows), f32),
            pltpu.VMEM((2, 4, chunks, width // HD, slot_rows), f32),
            pltpu.VMEM((heads, HD, rows), bf16),
            pltpu.VMEM((heads, rows), f32),
            dma((chunks, 2)), dma((3, chunks, 2)), dma((4, chunks, 2)), dma((3, 4, chunks)),
            dma((4, chunks)), dma((2, 2, chunks)),
            dma((4, chunks)), dma((2, 2, chunks)), dma((2, 4, chunks)),
            dma((4, chunks)), dma((2, 2, chunks)), dma((2, 4, chunks)),
        ],
        compiler_params=pltpu.CompilerParams(
            collective_id=0, has_side_effects=True, vmem_limit_bytes=56 * 1024 * 1024
        ),
        cost_estimate=pl.CostEstimate(
            flops=4 * work, bytes_accessed=12 * rows * columns, transcendentals=work // HD
        ),
    )(queries, cache_keys, cache_values, new_keys, new_values, packed, spreads)


def attend(query_rows, key_rows, value_rows, visible):
    partials = []
    log_totals = []
    for head_number in range(query_rows.shape[1]):
        scores = lax.dot_general(
            query_rows[:, head_number],
            key_rows[:, head_number],
            (((1,), (1,)), ((), ())),
            preferred_element_type=jnp.float32,
        ) / math.sqrt(HD)
        if visible is not None:
            scores = jnp.where(visible, scores, jnp.float32(-1e30))
        row_max = jnp.max(scores, axis=-1, keepdims=True)
        weights = jnp.exp(scores - row_max)
        row_total = jnp.sum(weights, axis=-1, keepdims=True)
        probs = (weights / row_total).astype(jnp.bfloat16)
        partial_value = jnp.dot(
            probs, value_rows[:, head_number], preferred_element_type=jnp.float32
        )
        partials.append(partial_value.astype(jnp.bfloat16))
        log_totals.append((row_max + jnp.log(row_total))[:, 0])
    return (jnp.stack(partials, axis=1), jnp.stack(log_totals, axis=1))


def pack_slots(queries, slot_index, live, slot_total, groups, ctx_size, capacity, head_count):
    pair_total = slot_index.shape[0]
    slot_pick = (
        (jnp.arange(slot_total, dtype=jnp.int32)[:, None] == slot_index[None, :]) & live[None, :]
    ).astype(jnp.bfloat16)
    pair_group = jnp.arange(pair_total, dtype=jnp.int32) // TOPK
    group_pick = (pair_group[:, None] == jnp.arange(groups, dtype=jnp.int32)[None, :]).astype(
        jnp.bfloat16
    )
    slot_group = jnp.dot(slot_pick, group_pick, preferred_element_type=jnp.float32).astype(
        jnp.bfloat16
    )
    outgoing = jnp.dot(slot_group, queries.reshape(groups, -1), preferred_element_type=jnp.float32)
    return outgoing.astype(jnp.bfloat16).reshape(ctx_size, capacity, QG, head_count, HD)


def exchanged_attention(queries, cache_keys, cache_values, new_keys, new_values, chosen):
    block_len = queries.shape[0]
    head_count = queries.shape[1] // HD
    groups = block_len // QG
    ctx_size = lax.axis_size("ctx")
    capacity = max(2, (groups * TOPK + ctx_size - 1) // ctx_size)
    query_rows = queries.reshape(block_len, head_count, HD)
    key_rows = cache_keys.reshape(block_len, head_count, HD)
    value_rows = cache_values.reshape(block_len, head_count, HD)
    target = chosen.reshape(-1)
    pair_total = target.shape[0]
    target_hit = (target[:, None] == jnp.arange(ctx_size, dtype=jnp.int32)[None, :]).astype(
        jnp.int32
    )
    before = jnp.sum((jnp.cumsum(target_hit, axis=0) - target_hit) * target_hit, axis=1)
    every_pair = jnp.ones((pair_total,), bool)
    slot_total = ctx_size * capacity
    slot_of = target * capacity + before
    outgoing = pack_slots(
        queries, slot_of, every_pair, slot_total, groups, ctx_size, capacity, head_count
    )
    incoming = lax.all_to_all(outgoing, "ctx", split_axis=0, concat_axis=0, tiled=True)
    item_count = incoming.shape[1]
    flat_rows = incoming.reshape(-1, head_count, HD)
    partial_value, log_total = attend(flat_rows, key_rows, value_rows, None)
    partial_value = partial_value.reshape(ctx_size, item_count, QG, head_count, HD)
    log_total = log_total.reshape(ctx_size, item_count, QG, head_count)
    partial_value, log_total = (partial_value, log_total)
    arrived = lax.all_to_all(
        partial_value.astype(jnp.float32), "ctx", split_axis=0, concat_axis=0, tiled=True
    ).astype(partial_value.dtype)
    arrived_log = lax.all_to_all(log_total, "ctx", split_axis=0, concat_axis=0, tiled=True)
    remote = jnp.take(arrived.reshape(slot_total, -1), slot_of, axis=0)
    remote_log = jnp.take(arrived_log.reshape(slot_total, -1), slot_of, axis=0)
    positions = jnp.arange(block_len, dtype=jnp.int32)
    visible = positions[:, None] >= positions[None, :]
    own_part, own_log = attend(
        query_rows,
        new_keys.reshape(block_len, head_count, HD),
        new_values.reshape(block_len, head_count, HD),
        visible,
    )
    remote = remote.reshape(groups, TOPK, QG, head_count, HD)
    remote_log = remote_log.reshape(groups, TOPK, QG, head_count)
    partials = jnp.concatenate([own_part.reshape(groups, 1, QG, head_count, HD), remote], axis=1)
    log_totals = jnp.concatenate([own_log.reshape(groups, 1, QG, head_count), remote_log], axis=1)
    top_log = jnp.max(log_totals, axis=1, keepdims=True)
    weights = jnp.exp(log_totals - top_log)
    row_total = jnp.sum(weights, axis=1)
    merged = (
        jnp.sum(weights[..., None] * partials.astype(jnp.float32), axis=1) / row_total[..., None]
    )
    merged = merged.astype(jnp.bfloat16).reshape(block_len, head_count * HD)
    return merged


def on_device(queries, cache_keys, cache_values, new_keys, new_values, chosen, out_weight):
    in_lines = lax.axis_size("ctx") == 8 and chosen.size * QG == 4 * queries.shape[0]
    attended = attention if in_lines else exchanged_attention
    merged = attended(queries, cache_keys, cache_values, new_keys, new_values, chosen)
    return project(merged, out_weight)


def solution(mesh):
    placed = (
        P("ctx", "head"),
        P("ctx", "head"),
        P("ctx", "head"),
        P("ctx", "head"),
        P("ctx", "head"),
        P("ctx", None),
        P("head", None),
    )
    return jax.shard_map(
        on_device, mesh=mesh, in_specs=placed, out_specs=P("ctx", "head"), check_vma=False
    )
```
